32 devices in a mesh: groups: 2 (over y), expert: 4 (over z), dp: 2 (over x), sub: 2 (over core).
Axes of the slice: x: 2, y: 2, z: 4, core: 2. Of those that a mesh axis runs over, the one named last changes fastest.
Arguments:
- tokens: bfloat16 [2048, 2048], P(('groups', 'expert', 'dp')), parts along dimension 0, may hold values from -6 to 6
- cotangent: bfloat16 [2048, 2048], P(('groups', 'expert', 'dp')), parts along dimension 0, may hold values from -6 to 6
- route_ids: int32 [2048, 4], P(('groups', 'expert', 'dp')), parts along dimension 0, may hold values from 0 to 15, all different within a row; in each aligned block of 128 rows (0 to 127, 128 to 255, ...) at most 36 rows name the same one
- route_weights: float32 [2048, 4], P(('groups', 'expert', 'dp')), parts along dimension 0, may hold values from 0.05 to 0.5
- w_gate: bfloat16 [16, 2048, 768], P('expert', 'dp', 'sub'), may hold values from -0.125 to 0.125
- w_up: bfloat16 [16, 2048, 768], P('expert', 'dp', 'sub'), may hold values from -0.125 to 0.125
- v_down: bfloat16 [32, 768, 2048], P(('groups', 'expert'), 'sub', 'dp'), parts along dimension 0, may hold values from -0.125 to 0.125
Outputs:
- grad_down: bfloat16 [32, 768, 2048], P(('groups', 'expert'), 'sub', 'dp'), parts along dimension 0
- hyper_tokens: bfloat16 [2048, 2048], P(('groups', 'expert', 'dp'), 'sub'), parts along dimension 0
The draws below stay inside these ranges and needn't reach their ends.
There are 2 independent parts, one for each index of `groups`. The reference program is written for one: setup_inputs(seed, part) draws one part's arguments, and reference() takes and returns one part's arrays. A program takes and returns all parts, laid end to end along the dimension named above; an argument that names none is the same for every part. Nothing has to cross between parts.
Inputs may be any that keep to these rules, and one draw needn't show every extreme that they name: `route_ids`: each token names 4 different experts. In the 128 rows of one token shard no expert is named by more than 36 tokens, a bound that some block reaches of them.
All inputs are finite; a program needn't handle non-finite values.
Results may differ from the reference program's by a relative error of at most 0.014.
Values may be sent and summed in bfloat16 or wider, within the bound.
No kernel may reach another device: no remote copies, remote signals or barrier semaphores. Data moves between devices by JAX's collectives and lax.ppermute only.
A program may use at most 128 MiB of HBM per device.

```python
import math
import jax
import jax.numpy as jnp
import numpy as np
from jax import lax

D = 2048
FF = 768
TOP = 4
TOK_DEV = 128
EXPERTS = 16
MOST = 36
TOKENS = 1024
N_EXPERT = 4
N_DP = 2


def level_of(stream_key, extent, pieces, low, high):
    factor_of, own = 1.0, jax.random.fold_in(stream_key, 6)
    for dim, parts in pieces:
        heights = jnp.exp(jax.random.uniform(jax.random.fold_in(own, dim), (parts,), jnp.float32, low / len(pieces), high / len(pieces)))
        factor_of = factor_of * jnp.repeat(heights, extent[dim] // parts).reshape([-1 if axis == dim else 1 for axis in range(len(extent))])
    return factor_of


def shared_out(stream_key, own, number, rows, count, top, bound, skew):
    order = jax.random.permutation(stream_key, count)
    crowded, common = shares(count, rows * top, bound, skew, True), shares(count, rows * top, bound, skew, False)
    places = jnp.arange(count)

    def named(lengths, rotation):
        used = int((lengths > 0).sum())
        fixed = max(1, used // 4)
        moved = fixed + (places - fixed + rotation * (used - fixed)) % max(1, count - fixed)
        return jnp.zeros((count,), jnp.int32).at[order[jnp.where(places < fixed, places, moved)]].set(jnp.asarray(lengths, jnp.int32))

    lengths = jnp.where(number % 4 == 0, named(crowded, number // 4), named(common, number - number // 4 - 1))
    mixed = jax.random.permutation(jax.random.fold_in(own, 3), count)
    giver, sink = mixed[0:count // 2 * 2:2], mixed[1:count // 2 * 2:2]
    slack = jnp.minimum(lengths[giver] - 1, bound - lengths[sink]) // 2
    slack = jnp.where((giver == order[0]) | (sink == order[0]) | (lengths[sink] == 0), 0, jnp.maximum(slack, 0))
    moved = jax.random.randint(jax.random.fold_in(own, 4), (count // 2,), 0, 1 << 20) % (slack + 1)
    lengths = lengths.at[giver].add(-moved).at[sink].add(moved)
    items = jnp.searchsorted(jnp.cumsum(lengths), jnp.arange(rows * top), side="right").astype(jnp.int32)
    listing = items.reshape(top, rows).T
    listing = listing[jax.random.permutation(jax.random.fold_in(own, 1), rows)]
    rotation = jax.random.randint(jax.random.fold_in(own, 2), (rows, 1), 0, top)
    return jnp.take_along_axis(listing, (jnp.arange(top)[None, :] + rotation) % top, axis=1)


def shares(count, total, bound, skew, full):
    portions = [(1 << 20) // math.isqrt(rank ** skew) + 1 for rank in range(1, count + 1)]
    largest = bound if full else min(bound, max(-(-total // count), total * portions[0] // sum(portions)))
    least = 1 if total - largest >= count - 1 else 0
    holding, spare = [largest] + [least] * (count - 1), total - largest - least * (count - 1)
    while spare > 0:
        candidates = [i for i in range(1, count) if holding[i] < largest] or [i for i in range(1, count) if holding[i] < bound]
        mass, budget = sum([portions[i] for i in candidates]), spare
        for i in candidates:
            extra = min(bound - holding[i], max(1, budget * portions[i] // mass), spare)
            holding[i] = holding[i] + extra
            spare = spare - extra
    return np.array(holding)


def bell_draw(own_key, shape, deviation, most, cuts=(), kind=jnp.bfloat16):
    drawn = deviation * jax.random.normal(own_key, shape, jnp.float32)
    if cuts:
        drawn = drawn * level_of(own_key, shape, cuts, -0.22, 0.18)
    return jnp.clip(drawn, -most, most).astype(kind)


def setup_inputs(seed: int = 0, part: int = 0) -> dict:
    key_list = jax.random.split(jax.random.key(seed), 8)
    part_splits = jax.random.split(jax.random.fold_in(key_list[7], part), 8)
    tokens = bell_draw(part_splits[0], (TOKENS, D), 1.0, 6.0, ((0, 8),))
    cotangent = bell_draw(part_splits[1], (TOKENS, D), 1.0, 6.0, ((0, 8),))
    route_ids_keys = jax.random.split(jax.random.fold_in(part_splits[2], 1), TOKENS // TOK_DEV)
    route_ids_turns = jax.random.permutation(jax.random.fold_in(part_splits[2], 3), TOKENS // TOK_DEV)
    route_ids = jax.vmap(lambda own, number: shared_out(jax.random.fold_in(part_splits[2], 2), own, number, TOK_DEV, EXPERTS, TOP, MOST, 2))(route_ids_keys, route_ids_turns).reshape((TOKENS, TOP))
    route_weights = jnp.clip(jnp.exp(math.log(0.5) - 2.3025851 * jax.random.uniform(part_splits[3], (TOKENS, TOP), jnp.float32) ** level_of(part_splits[3], (TOKENS, TOP), ((0, 8),), -0.2, 0.2)), 0.05, 0.5)
    w_gate = bell_draw(key_list[4], (EXPERTS, D, FF), D ** -0.5, 0.125, ((0, 4), (1, 2), (2, 2)))
    w_up = bell_draw(key_list[5], (EXPERTS, D, FF), D ** -0.5, 0.125, ((0, 4), (1, 2), (2, 2)))
    v_down = bell_draw(part_splits[6], (EXPERTS, FF, D), D ** -0.5, 0.125, ((0, 4), (1, 2), (2, 2)))
    return dict(tokens=tokens, cotangent=cotangent, route_ids=route_ids, route_weights=route_weights, w_gate=w_gate, w_up=w_up, v_down=v_down)


def slot_positions(chosen_ids, expert_count, capacity):
    flat_ids = chosen_ids.reshape(-1)
    onehot = (flat_ids[:, None] == jnp.arange(expert_count, dtype=jnp.int32)[None, :]).astype(jnp.int32)
    earlier = jnp.cumsum(onehot, axis=0) - onehot
    rank_in = jnp.sum(earlier * onehot, axis=1)
    return (flat_ids * capacity + rank_in).reshape(chosen_ids.shape).astype(jnp.int32)


def reference(tokens, cotangent, route_ids, route_weights, w_gate, w_up, v_down):
    shards = N_EXPERT * N_DP
    shard_ids = route_ids.reshape(shards, TOK_DEV, TOP)
    slot_index = jax.vmap(lambda block: slot_positions(block, EXPERTS, MOST))(shard_ids)
    shard_rows = jnp.arange(shards, dtype=jnp.int32)[:, None, None] * jnp.ones_like(slot_index)
    token_rows = jnp.arange(TOKENS, dtype=jnp.int32).reshape(shards, TOK_DEV, 1) * jnp.ones_like(slot_index)
    slot_table = jnp.full((shards, EXPERTS * MOST), TOKENS, jnp.int32).at[shard_rows, slot_index].set(token_rows)
    scale_table = jnp.zeros((shards, EXPERTS * MOST), jnp.float32).at[shard_rows, slot_index].set(
        route_weights.reshape(shards, TOK_DEV, TOP))
    slot_table = slot_table.reshape(shards, EXPERTS, MOST).transpose(1, 0, 2).reshape(EXPERTS, shards * MOST)
    scale_table = scale_table.reshape(shards, EXPERTS, MOST).transpose(1, 0, 2).reshape(EXPERTS, shards * MOST)
    padded_tokens = jnp.concatenate([tokens, jnp.zeros((1, D), jnp.bfloat16)], axis=0)
    padded_cotangent = jnp.concatenate([cotangent, jnp.zeros((1, D), jnp.bfloat16)], axis=0)

    def expert_step(hyper_rows, inputs):
        gate_block, up_block, tangent_block, row_index, row_scales = inputs
        token_block = padded_tokens[row_index]
        cot_block = padded_cotangent[row_index]
        pre_gate = jnp.dot(token_block, gate_block, preferred_element_type=jnp.float32)
        pre_up = jnp.dot(token_block, up_block, preferred_element_type=jnp.float32)
        tangent = jnp.dot(cot_block, tangent_block.T, preferred_element_type=jnp.float32)
        sigmoid_gate = jax.nn.sigmoid(pre_gate)
        activated = pre_gate * sigmoid_gate
        slope = sigmoid_gate * (1.0 + pre_gate * (1.0 - sigmoid_gate))
        weighting = row_scales[:, None]
        weighted_hidden = (weighting * activated * pre_up).astype(jnp.bfloat16)
        per_index = jnp.einsum("admf,admk->dfk",
                               weighted_hidden.reshape(N_EXPERT, N_DP, MOST, FF).astype(jnp.float32),
                               cot_block.reshape(N_EXPERT, N_DP, MOST, D).astype(jnp.float32))
        rounded = lax.optimization_barrier(per_index.astype(jnp.bfloat16))
        grad_block = jnp.sum(rounded.astype(jnp.float32), axis=0).astype(jnp.bfloat16)
        scaled_tangent = weighting * tangent
        gate_adjoint = (scaled_tangent * pre_up * slope).astype(jnp.bfloat16)
        up_adjoint = (scaled_tangent * activated).astype(jnp.bfloat16)
        partial_value = jnp.dot(gate_adjoint, gate_block.T, preferred_element_type=jnp.float32)
        partial_value = partial_value + jnp.dot(up_adjoint, up_block.T, preferred_element_type=jnp.float32)
        hyper_rows = hyper_rows.at[row_index].add(partial_value)
        return hyper_rows, grad_block

    hyper_rows, grad_down = lax.scan(expert_step, jnp.zeros((TOKENS + 1, D), jnp.float32),
                                     (w_gate, w_up, v_down, slot_table, scale_table))
    return grad_down, hyper_rows[:TOKENS].astype(jnp.bfloat16)
```

```python
import functools

import jax
import jax.numpy as jnp
from jax import lax
from jax.experimental import pallas as pl
from jax.experimental.pallas import tpu as pltpu
from jax.sharding import PartitionSpec as P

BF = jnp.bfloat16
F32 = jnp.float32
LANES = 128
VMEM_LIMIT = 48 * 1024 * 1024


def up_to(value, step):
    return -(-value // step) * step


def dot(a, b, contract=((1,), (0,))):
    return lax.dot_general(a, b, (contract, ((), ())), preferred_element_type=F32)


def vmem_spec(shape):
    return pl.BlockSpec(shape, lambda j: (0,) * len(shape))


def expert_spec(shape):
    return pl.BlockSpec((1,) + shape, lambda j: (j,) + (0,) * len(shape))


def route_tables(payload, token_rows, chosen, first_expert, local_experts, tables):
    shards = payload.shape[0]
    width = token_rows // LANES
    per_row = payload.shape[2] // LANES

    def entry(index):
        pieces = []
        for shard in range(shards):
            for piece in range(width):
                row, column = divmod(index * width + piece, per_row)
                pieces.append(
                    payload[shard, token_rows:, :].astype(F32)[
                        row : row + 1, column * LANES : (column + 1) * LANES
                    ]
                )
        return jnp.concatenate(pieces, axis=1)

    ids = [entry(k) for k in range(chosen)]
    weights = [
        entry(chosen + k) + entry(2 * chosen + k) + entry(3 * chosen + k) for k in range(chosen)
    ]
    total = shards * token_rows
    masks, scales = [], []
    for local in range(local_experts):
        wanted = (first_expert + local).astype(F32)
        hits = [(one == wanted).astype(F32) for one in ids]
        masks.append(sum(hits))
        scales.append(sum(hit * weight for hit, weight in zip(hits, weights)))
    pad = [jnp.zeros((8 - local_experts, total), F32)] if local_experts < 8 else []
    mask = jnp.concatenate(masks + pad, axis=0)
    before = lax.broadcasted_iota(jnp.int32, (total, total), 0) < lax.broadcasted_iota(
        jnp.int32, (total, total), 1
    )
    rank = dot(mask.astype(BF), before.astype(F32).astype(BF))
    tables[0:8, :] = jnp.where(mask > 0.5, rank, -1.0)
    tables[8:16, :] = jnp.concatenate(scales + pad, axis=0)


def one_hot(tables, local, slots):
    rank = tables[pl.ds(local, 1), :].astype(jnp.int32)
    total = rank.shape[1]
    return lax.broadcasted_iota(jnp.int32, (slots, total), 0) == rank


def forward_kernel(
    token_rows, chosen, capacity, place, mine, other, gate, up, down, sums, cot_rows, tables,
    token_scratch, sum_scratch,
):
    local = pl.program_id(0)
    shards = mine.shape[0]
    quarter = mine.shape[2] // 2
    slots = token_scratch.shape[0]

    @pl.when(local == 0)
    def _():
        route_tables(mine, token_rows, chosen, place[1], pl.num_programs(0), tables)

    hot = one_hot(tables, local, slots).astype(F32).astype(BF)
    for source, which in ((mine, place[0]), (other, 1 - place[0])):
        rows = source[:, 0:token_rows, :].reshape(shards * token_rows, 2 * quarter)
        picked = dot(hot, rows).astype(BF)
        columns = pl.ds(pl.multiple_of(which * quarter, LANES), quarter)
        token_scratch[:, columns] = picked[:, :quarter]
        cot_rows[0, :, columns] = picked[:, quarter:]
    here = pl.ds(pl.multiple_of(local * capacity, 8), capacity)
    sum_scratch[0, here, :] = dot(token_scratch[...], gate[0])[:capacity]
    sum_scratch[1, here, :] = dot(token_scratch[...], up[0])[:capacity]
    sum_scratch[2, here, :] = dot(cot_rows[0], down[0], ((1,), (1,)))[:capacity]

    @pl.when(local == pl.num_programs(0) - 1)
    def _():
        sums[...] = sum_scratch[...].astype(BF)


def backward_kernel(capacity, place, tables, *refs):
    *sums, gate, up, hidden, keep, send, full, total = refs
    local = pl.program_id(0)
    rows = sums[0].shape[1]
    slots = hidden.shape[1]
    quarter = keep.shape[1]

    @pl.when(local == 0)
    def _():
        full[:, 0:rows, :] = sum(one[...].astype(F32) for one in sums)
        full[:, rows:, :] = jnp.zeros((3, full.shape[1] - rows, full.shape[2]), F32)
        total[...] = jnp.zeros_like(total)

    hot = one_hot(tables, local, slots).astype(F32)
    scale = jnp.sum(hot * tables[pl.ds(8 + local, 1), :], axis=1, keepdims=True)
    here = pl.ds(pl.multiple_of(local * capacity, 8), slots)
    pre_gate, pre_up, tangent = full[0, here, :], full[1, here, :], full[2, here, :]
    sigmoid_gate = jax.nn.sigmoid(pre_gate)
    act = pre_gate * sigmoid_gate
    slope = sigmoid_gate * (1.0 + pre_gate * (1.0 - sigmoid_gate))
    hidden[0] = (scale * act * pre_up).astype(BF)
    scaled = scale * tangent
    gate_adjoint = (scaled * pre_up * slope).astype(BF)
    up_adjoint = (scaled * act).astype(BF)
    hot = hot.astype(BF)
    gate_tokens = dot(hot, gate_adjoint, ((0,), (0,))).astype(BF)
    up_tokens = dot(hot, up_adjoint, ((0,), (0,))).astype(BF)
    total[...] += dot(gate_tokens, gate[0], ((1,), (1,))) + dot(up_tokens, up[0], ((1,), (1,)))

    @pl.when(local == pl.num_programs(0) - 1)
    def _():
        for out, which in ((keep, place[0]), (send, 1 - place[0])):
            out[...] = total[:, pl.ds(pl.multiple_of(which * quarter, LANES), quarter)].astype(BF)


def grad_kernel(*refs):
    *inputs, out = refs
    half = len(inputs) // 2
    hidden = jnp.concatenate([one[0] for one in inputs[:half]], axis=0)
    cot_rows = jnp.concatenate([one[0] for one in inputs[half:]], axis=0)
    out[0] = dot(hidden, cot_rows, ((0,), (0,))).astype(BF)


def params():
    return pltpu.CompilerParams(
        vmem_limit_bytes=VMEM_LIMIT, dimension_semantics=("arbitrary",)
    )


SMEM = pl.BlockSpec(memory_space=pltpu.SMEM)


def forward(place, mine, other, gate, up, down, token_rows, chosen, capacity):
    local_experts, depth, hidden = gate.shape
    slots = up_to(capacity, 16)
    rows = local_experts * capacity
    tokens = mine.shape[0] * token_rows
    return pl.pallas_call(
        functools.partial(forward_kernel, token_rows, chosen, capacity),
        grid=(local_experts,),
        in_specs=[
            SMEM,
            vmem_spec(mine.shape),
            vmem_spec(other.shape),
            expert_spec((depth, hidden)),
            expert_spec((depth, hidden)),
            expert_spec((hidden, depth)),
        ],
        out_specs=[
            vmem_spec((3, rows, hidden)),
            expert_spec((slots, depth)),
            vmem_spec((16, tokens)),
        ],
        out_shape=[
            jax.ShapeDtypeStruct((3, rows, hidden), BF),
            jax.ShapeDtypeStruct((local_experts, slots, depth), BF),
            jax.ShapeDtypeStruct((16, tokens), F32),
        ],
        scratch_shapes=[pltpu.VMEM((slots, depth), BF), pltpu.VMEM((3, rows, hidden), F32)],
        compiler_params=params(),
        cost_estimate=pl.CostEstimate(
            flops=2 * local_experts * slots * depth * (3 * hidden + 2 * tokens),
            bytes_accessed=2 * (3 * gate.size + 2 * mine.size + 3 * rows * hidden),
            transcendentals=0,
        ),
    )(place, mine, other, gate, up, down)


def backward(place, tables, sums, gate, up, capacity):
    local_experts, depth, hidden = gate.shape
    slots = up_to(capacity, 16)
    tokens = tables.shape[1]
    return pl.pallas_call(
        functools.partial(backward_kernel, capacity),
        grid=(local_experts,),
        in_specs=[SMEM, vmem_spec(tables.shape)]
        + [vmem_spec(one.shape) for one in sums]
        + [expert_spec((depth, hidden))] * 2,
        out_specs=[
            expert_spec((slots, hidden)),
            vmem_spec((tokens, depth // 2)),
            vmem_spec((tokens, depth // 2)),
        ],
        out_shape=[
            jax.ShapeDtypeStruct((local_experts, slots, hidden), BF),
            jax.ShapeDtypeStruct((tokens, depth // 2), BF),
            jax.ShapeDtypeStruct((tokens, depth // 2), BF),
        ],
        scratch_shapes=[
            pltpu.VMEM((3, sums[0].shape[1] + slots - capacity + 8, hidden), F32),
            pltpu.VMEM((tokens, depth), F32),
        ],
        compiler_params=params(),
        cost_estimate=pl.CostEstimate(
            flops=4 * local_experts * tokens * hidden * (depth + slots),
            bytes_accessed=2 * (2 * gate.size + 6 * sums[0].size),
            transcendentals=sums[0].size,
        ),
    )(place, tables, *sums, gate, up)


def grads(hiddens, cots):
    local_experts, slots, hidden = hiddens[0].shape
    depth = cots[0].shape[2]
    return pl.pallas_call(
        grad_kernel,
        grid=(local_experts,),
        in_specs=[expert_spec((slots, hidden))] * len(hiddens)
        + [expert_spec((slots, depth))] * len(cots),
        out_specs=expert_spec((hidden, depth)),
        out_shape=jax.ShapeDtypeStruct((local_experts, hidden, depth), BF),
        compiler_params=params(),
        cost_estimate=pl.CostEstimate(
            flops=2 * local_experts * slots * len(cots) * hidden * depth,
            bytes_accessed=2 * local_experts * (hidden * depth + len(cots) * slots * depth),
            transcendentals=0,
        ),
    )(*hiddens, *cots)


def shift(array, axis, by):
    size = lax.axis_size(axis)
    return lax.ppermute(array, axis, [(i, (i + by) % size) for i in range(size)])


def per_device(tokens, cotangent, route_ids, route_weights, w_gate, w_up, v_down):
    owners, wide, cores = (lax.axis_size(a) for a in ("expert", "dp", "sub"))
    owner, dp, sub = (lax.axis_index(a) for a in ("expert", "dp", "sub"))
    token_rows, chosen = route_ids.shape
    local_experts = w_gate.shape[0]
    expert_count = owners * local_experts
    most = max(2, 9 * token_rows * chosen // (8 * expert_count))
    capacity = up_to(wide * most, 8)
    quarter = tokens.shape[1] // (wide * cores)
    place = jnp.stack([sub, owner * local_experts]).astype(jnp.int32)

    parts, rest = [], route_weights
    for _ in range(3):
        part = lax.reduce_precision(rest, 8, 7)
        parts.append(part)
        rest = rest - part
    routing = jnp.concatenate([route_ids.astype(F32)] + parts, axis=1).astype(BF).T
    routing = routing.reshape(-1)
    routing = jnp.pad(routing, (0, -routing.shape[0] % (4 * quarter))).reshape(-1, 2 * quarter)

    def payload(to):
        start = (to * cores + sub) * quarter
        body = jnp.concatenate(
            [lax.dynamic_slice_in_dim(a, start, quarter, 1) for a in (tokens, cotangent)], axis=1
        )
        return jnp.concatenate([body, routing], axis=0)[None]

    mine = jnp.zeros((wide, token_rows + routing.shape[0], 2 * quarter), BF)
    mine = lax.dynamic_update_slice_in_dim(mine, payload(dp), dp, 0)
    for by in range(1, wide):
        got = shift(payload((dp + by) % wide), "dp", by)
        mine = lax.dynamic_update_slice_in_dim(mine, got, (dp - by) % wide, 0)

    order = sorted(range(owners), key=lambda by: min(by, owners - by))
    blocks = [mine if by == 0 else shift(mine, "expert", by) for by in order]
    total, hiddens, cots = None, [], []
    for by, block in zip(order, blocks):
        other = shift(block, "sub", 1)
        sums, cot_rows, tables = forward(
            place, block, other, w_gate, w_up, v_down, token_rows, chosen, capacity
        )
        everyone = [sums] + [shift(sums, "dp", step) for step in range(1, wide)]
        hidden, keep, send = backward(place, tables, everyone, w_gate, w_up, capacity)
        hiddens.append(hidden)
        cots.append(cot_rows)
        rows = keep.astype(F32) + shift(send, "sub", 1).astype(F32)
        if by:
            rows = shift(rows.astype(BF), "expert", -by).astype(F32)
        total = rows if total is None else total + rows
    grad_down = grads(hiddens, cots)

    total = total.astype(BF).reshape(wide, token_rows, quarter)
    pieces = jnp.zeros_like(total)
    pieces = lax.dynamic_update_slice_in_dim(
        pieces, lax.dynamic_slice_in_dim(total, dp, 1, 0), dp, 0
    )
    for by in range(1, wide):
        got = shift(lax.dynamic_slice_in_dim(total, (dp + by) % wide, 1, 0), "dp", by)
        pieces = lax.dynamic_update_slice_in_dim(pieces, got, (dp - by) % wide, 0)
    span = wide // cores
    stay = lax.dynamic_slice_in_dim(pieces, sub * span, span, 0)
    come = shift(lax.dynamic_slice_in_dim(pieces, (1 - sub) * span, span, 0), "sub", 1)
    columns = []
    for index in range(span):
        columns.append(jnp.where(sub == 0, stay[index], come[index]))
        columns.append(jnp.where(sub == 0, come[index], stay[index]))
    return (grad_down, jnp.concatenate(columns, axis=1))


def solution(mesh):
    placed = (
        P(("groups", "expert", "dp"), None),
        P(("groups", "expert", "dp"), None),
        P(("groups", "expert", "dp"), None),
        P(("groups", "expert", "dp"), None),
        P("expert", "dp", "sub"),
        P("expert", "dp", "sub"),
        P(("groups", "expert"), "sub", "dp"),
    )
    return jax.shard_map(
        per_device,
        mesh=mesh,
        in_specs=placed,
        out_specs=(P(("groups", "expert"), "sub", "dp"), P(("groups", "expert", "dp"), "sub")),
        check_vma=False,
    )
```

```python
import functools

import jax
import jax.numpy as jnp
from jax import lax
from jax.experimental import pallas as pl
from jax.experimental.pallas import tpu as pltpu
from jax.sharding import PartitionSpec as P

BF = jnp.bfloat16
F32 = jnp.float32
LANES = 128


def up_to(value, step):
    return -(-value // step) * step


def dot(a, b, contract=((1,), (0,))):
    return lax.dot_general(a, b, (contract, ((), ())), preferred_element_type=F32)


def vmem_spec(shape):
    return pl.BlockSpec(shape, lambda j: (0,) * len(shape))


def expert_spec(shape):
    return pl.BlockSpec((1,) + shape, lambda j: (j,) + (0,) * len(shape))


def pack_kernel(place, tokens, cotangent, route_ids, route_weights, *refs):
    *outs, ids, weights, sems = refs
    chosen, rows = ids.shape
    quarter = outs[0].shape[1] // 2
    wide = len(outs) - 1
    dp, sub = place[2], place[0]
    copies = [
        pltpu.make_async_copy(route_ids, ids, sems.at[0]),
        pltpu.make_async_copy(route_weights, weights, sems.at[1]),
    ]
    wanted = [((dp + by) % wide, sub) for by in range(1, wide)] + [(dp, sub), (dp, 1 - sub)]
    for out, (half, which) in zip(outs, wanted):
        columns = pl.ds(pl.multiple_of((half * 2 + which) * quarter, LANES), quarter)
        for source, at in ((tokens, 0), (cotangent, quarter)):
            target = out.at[0:rows, at : at + quarter]
            copies.append(
                pltpu.make_async_copy(source.at[:, columns], target, sems.at[len(copies)])
            )
    for copy in copies:
        copy.start()
    copies[0].wait()
    copies[1].wait()
    parts, rest = [ids[...].astype(F32)], weights[...]
    for _ in range(3):
        part = rest.astype(BF).astype(F32)
        parts.append(part)
        rest = rest - part
    table = jnp.concatenate(parts, axis=0)
    per_row = 2 * quarter // rows
    lines = [
        jnp.concatenate([table[i : i + 1] for i in range(start, start + per_row)], axis=1)
        for start in range(0, 4 * chosen, per_row)
    ]
    lines.append(jnp.zeros((ROUTE_ROWS - len(lines), 2 * quarter), F32))
    lines = jnp.concatenate(lines, axis=0).astype(BF)
    for out in outs:
        out[rows:, :] = lines
    for copy in copies[2:]:
        copy.wait()


def pack(place, tokens, cotangent, route_ids, route_weights, wide, quarter):
    rows, chosen = route_ids.shape
    shape = (rows + ROUTE_ROWS, 2 * quarter)
    return pl.pallas_call(
        pack_kernel,
        in_specs=[SMEM] + [pl.BlockSpec(memory_space=pltpu.HBM)] * 4,
        out_specs=[WHOLE] * (wide + 1),
        out_shape=[jax.ShapeDtypeStruct(shape, BF)] * (wide + 1),
        scratch_shapes=[
            pltpu.VMEM((chosen, rows), jnp.int32),
            pltpu.VMEM((chosen, rows), F32),
            pltpu.SemaphoreType.DMA((2 * wide + 4,)),
        ],
        compiler_params=pltpu.CompilerParams(vmem_limit_bytes=LIMIT),
        cost_estimate=PACK_COST,
    )(place, tokens, cotangent, route_ids.T, route_weights.T)


def route_tables(payloads, token_rows, chosen, first_expert, dp, local_experts, tables):
    shards = len(payloads)
    per_row = payloads[0].shape[1] // token_rows
    lines = [payload[token_rows:, :].astype(F32) for payload in payloads]

    def entry(index):
        row, column = divmod(index, per_row)
        at = slice(column * token_rows, (column + 1) * token_rows)
        return jnp.concatenate([line[row : row + 1, at] for line in lines], axis=1)

    ids = [entry(k) for k in range(chosen)]
    weights = [
        entry(chosen + k) + entry(2 * chosen + k) + entry(3 * chosen + k) for k in range(chosen)
    ]
    total = shards * token_rows
    masks, scales = [], []
    for local in range(local_experts):
        wanted = (first_expert + local).astype(F32)
        hits = [(one == wanted).astype(F32) for one in ids]
        masks.append(sum(hits))
        scales.append(sum(hit * weight for hit, weight in zip(hits, weights)))
    pad = [jnp.zeros((8 - local_experts, total), F32)] if local_experts < 8 else []
    mask = jnp.concatenate(masks + pad, axis=0)

    def number(axis):
        index = lax.broadcasted_iota(jnp.int32, (total, total), axis)
        part = sum((index >= i * token_rows).astype(jnp.int32) for i in range(1, shards + 1))
        shard = dp - part
        return index + (jnp.where(shard < 0, shard + shards, shard) - part) * token_rows

    rank = dot(mask.astype(BF), (number(0) < number(1)).astype(F32).astype(BF))
    tables[0:8, :] = jnp.where(mask > 0.5, rank, -1.0)
    tables[8:16, :] = jnp.concatenate(scales + pad, axis=0)


def one_hot(tables, local, slots):
    rank = tables[pl.ds(local, 1), :].astype(jnp.int32)
    total = rank.shape[1]
    return lax.broadcasted_iota(jnp.int32, (slots, total), 0) == rank


def forward_kernel(shards, token_rows, chosen, capacity, streamed, place, *refs):
    mine, other, refs = refs[:shards], refs[shards : 2 * shards], refs[2 * shards :]
    gate, up, down, _, sums, cot_rows, tables, token_scratch, sum_scratch = refs
    quarter = mine[0].shape[1] // 2
    experts = sums.shape[1] // capacity
    slots = cot_rows.shape[1]

    def routing():
        route_tables(mine, token_rows, chosen, place[1], place[2], experts, tables)

    def finish():
        sums[...] = sum_scratch[...].astype(BF)

    def one_expert(local, at):
        hot = one_hot(tables, local, slots).astype(F32).astype(BF)
        for source, which in ((mine, place[0]), (other, 1 - place[0])):
            rows = jnp.concatenate([one[0:token_rows, :] for one in source], axis=0)
            columns = pl.ds(pl.multiple_of(which * quarter, LANES), quarter)
            picked = dot(hot, rows).astype(BF)
            token_scratch[:, columns] = picked[:, :quarter]
            cot_rows[at, :, columns] = picked[:, quarter:]
        start = pl.multiple_of(local * capacity, 8) if streamed else local * capacity
        here = pl.ds(start, capacity)
        sum_scratch[0, here, :] = dot(token_scratch[...], gate[at])[:capacity]
        sum_scratch[1, here, :] = dot(token_scratch[...], up[at])[:capacity]
        sum_scratch[2, here, :] = dot(cot_rows[at], down[at], ((1,), (1,)))[:capacity]

    if streamed:
        local = pl.program_id(0)
        pl.when(local == 0)(routing)
        one_expert(local, 0)
        pl.when(local == experts - 1)(finish)
    else:
        routing()
        for local in range(experts):
            one_expert(local, local)
        finish()


def backward_kernel(capacity, parts, wide, place, *refs):
    tables, refs = refs[:parts], refs[parts:]
    sums, refs = refs[: parts * wide], refs[parts * wide :]
    gate, up, _, hidden, keep, send, full, total = refs
    rows = sums[0].shape[1]
    experts = hidden.shape[0]
    slots = hidden.shape[1] // parts
    quarter = keep.shape[1]
    for part in range(parts):
        here = sums[part * wide : (part + 1) * wide]
        full[part, :, 0:rows, :] = sum(one[...].astype(F32) for one in here)
        full[part, :, rows:, :] = jnp.zeros((3, full.shape[2] - rows, full.shape[3]), F32)
    for local in range(experts):
        gate_tokens, up_tokens = [], []
        for part in range(parts):
            hot = one_hot(tables[part], local, slots).astype(F32)
            scale = jnp.sum(hot * tables[part][8 + local : 9 + local, :], axis=1, keepdims=True)
            here = slice(local * capacity, local * capacity + slots)
            pre_gate, pre_up, tangent = (full[part, i, here, :] for i in range(3))
            sigmoid_gate = jax.nn.sigmoid(pre_gate)
            act = pre_gate * sigmoid_gate
            slope = sigmoid_gate * (1.0 + pre_gate * (1.0 - sigmoid_gate))
            hidden[local, part * slots : (part + 1) * slots, :] = (scale * act * pre_up).astype(BF)
            scaled = scale * tangent
            gate_adjoint = (scaled * pre_up * slope).astype(BF)
            up_adjoint = (scaled * act).astype(BF)
            hot = hot.astype(BF)
            gate_tokens.append(dot(hot, gate_adjoint, ((0,), (0,))).astype(BF))
            up_tokens.append(dot(hot, up_adjoint, ((0,), (0,))).astype(BF))
        gate_tokens = jnp.concatenate(gate_tokens, axis=0)
        up_tokens = jnp.concatenate(up_tokens, axis=0)
        term = dot(gate_tokens, gate[local], ((1,), (1,)))
        term = term + dot(up_tokens, up[local], ((1,), (1,)))
        total[...] = term if local == 0 else total[...] + term
    for out, which in ((keep, place[0]), (send, 1 - place[0])):
        out[...] = total[:, pl.ds(pl.multiple_of(which * quarter, LANES), quarter)].astype(BF)


def grad_kernel(half, *refs):
    *inputs, out, done = refs
    done[...] = jnp.zeros_like(done)
    local = pl.program_id(0)
    hidden = jnp.concatenate([one[local] for one in inputs[:half]], axis=0)
    cot_rows = jnp.concatenate([one[local] for one in inputs[half:]], axis=0)
    out[0] = dot(hidden, cot_rows, ((0,), (0,))).astype(BF)


SMEM = pl.BlockSpec(memory_space=pltpu.SMEM)
ANY = pl.BlockSpec(memory_space=pl.ANY)
WHOLE = pl.BlockSpec(memory_space=pltpu.VMEM)
LIMIT = 12 * 1024 * 1024
STREAM_LIMIT = 60 * 1024 * 1024
ROUTE_ROWS = 16
PACK_COST = pl.CostEstimate(flops=1, bytes_accessed=32 * 1024 * 1024, transcendentals=0)
NO_COST = pl.CostEstimate(flops=1, bytes_accessed=1, transcendentals=0)


def forward(
    place, mine, other, gate, up, down, token_rows, chosen, most, previous, streamed=False
):
    local_experts, depth, hidden = gate.shape
    shards = len(mine)
    capacity = up_to(shards * most, 8)
    slots = up_to(capacity, 16)
    rows = local_experts * capacity
    tokens = shards * token_rows
    weights = [WHOLE] * 3
    if streamed:
        weights = [expert_spec((depth, hidden))] * 2 + [expert_spec((hidden, depth))]
    return pl.pallas_call(
        functools.partial(forward_kernel, shards, token_rows, chosen, capacity, streamed),
        grid=(local_experts,) if streamed else (),
        in_specs=[SMEM] + [WHOLE] * (2 * shards) + weights + [ANY],
        out_specs=[WHOLE, expert_spec((slots, depth)) if streamed else WHOLE, WHOLE],
        out_shape=[
            jax.ShapeDtypeStruct((3, rows, hidden), BF),
            jax.ShapeDtypeStruct((local_experts, slots, depth), BF),
            jax.ShapeDtypeStruct((16, tokens), F32),
        ],
        scratch_shapes=[pltpu.VMEM((slots, depth), BF), pltpu.VMEM((3, rows, hidden), F32)],
        compiler_params=pltpu.CompilerParams(vmem_limit_bytes=STREAM_LIMIT if streamed else LIMIT),
        cost_estimate=NO_COST,
    )(place, *mine, *other, gate, up, down, previous)


def backward(place, tables, sums, gate, up, previous):
    local_experts, depth, hidden = gate.shape
    parts, wide = len(tables), len(sums[0])
    rows = sums[0][0].shape[1]
    capacity = rows // local_experts
    slots = up_to(capacity, 16)
    tokens = parts * tables[0].shape[1]
    flat = [one for part in sums for one in part]
    return pl.pallas_call(
        functools.partial(backward_kernel, capacity, parts, wide),
        in_specs=[SMEM] + [WHOLE] * (parts + len(flat) + 2) + [ANY],
        out_specs=[WHOLE] * 3,
        out_shape=[
            jax.ShapeDtypeStruct((local_experts, parts * slots, hidden), BF),
            jax.ShapeDtypeStruct((tokens, depth // 2), BF),
            jax.ShapeDtypeStruct((tokens, depth // 2), BF),
        ],
        scratch_shapes=[
            pltpu.VMEM((parts, 3, rows + slots - capacity + 8, hidden), F32),
            pltpu.VMEM((tokens, depth), F32),
        ],
        compiler_params=pltpu.CompilerParams(vmem_limit_bytes=LIMIT),
        cost_estimate=NO_COST,
    )(place, *tables, *flat, gate, up, previous)


def grads(hiddens, cots):
    local_experts, _, hidden = hiddens[0].shape
    depth = cots[0].shape[2]
    slots = sum(one.shape[1] for one in cots)
    return pl.pallas_call(
        functools.partial(grad_kernel, len(hiddens)),
        grid=(local_experts,),
        in_specs=[WHOLE] * (len(hiddens) + len(cots)),
        out_specs=[expert_spec((hidden, depth)), vmem_spec((8, LANES))],
        out_shape=[
            jax.ShapeDtypeStruct((local_experts, hidden, depth), BF),
            jax.ShapeDtypeStruct((8, LANES), F32),
        ],
        compiler_params=pltpu.CompilerParams(vmem_limit_bytes=LIMIT),
        cost_estimate=NO_COST,
    )(*hiddens, *cots)


def small(kernel, shapes, *arrays):
    return pl.pallas_call(
        kernel,
        in_specs=[SMEM] + [WHOLE] * (len(arrays) - 1),
        out_specs=[WHOLE] * len(shapes),
        out_shape=[jax.ShapeDtypeStruct(shape, BF) for shape in shapes],
        compiler_params=pltpu.CompilerParams(vmem_limit_bytes=LIMIT),
        cost_estimate=NO_COST,
    )(*arrays)


def sum_kernel(inputs, place, *refs):
    total = sum(one[...].astype(F32) for one in refs[:inputs]).astype(BF)
    rows = refs[inputs].shape[0]
    for index, out in enumerate(refs[inputs:]):
        out[...] = total[index * rows : (index + 1) * rows]


def turned_kernel(inputs, place, *refs):
    total = sum(one[...].astype(F32) for one in refs[:inputs]).astype(BF)
    first, second = refs[inputs:]
    rows = first.shape[0]
    straight = place[2] == place[0]

    @pl.when(straight)
    def _():
        first[...] = total[:rows]
        second[...] = total[rows:]

    @pl.when(jnp.logical_not(straight))
    def _():
        first[...] = total[rows:]
        second[...] = total[:rows]


def choose_kernel(place, one, two, stay, send):
    straight = place[2] == place[0]

    @pl.when(straight)
    def _():
        stay[...] = one[...]
        send[...] = two[...]

    @pl.when(jnp.logical_not(straight))
    def _():
        stay[...] = two[...]
        send[...] = one[...]


def final_kernel(place, stay, come, *refs):
    *far, out = refs
    quarter = stay.shape[1]

    def far_sum(flip):
        return [
            sum(far[start + (q + flip) % 2][...].astype(F32) for start in range(0, len(far), 2))
            for q in range(2)
        ]

    for sub in range(2):
        for dp in range(2):

            @pl.when((place[0] == sub) & (place[2] == dp))
            def _():
                own = [stay[...], come[...]] if sub == 0 else [come[...], stay[...]]
                for q, extra in enumerate(far_sum(dp)):
                    out[:, q * quarter : (q + 1) * quarter] = (own[q].astype(F32) + extra).astype(BF)


def shift(array, axis, by):
    size = lax.axis_size(axis)
    return lax.ppermute(array, axis, [(i, (i + by) % size) for i in range(size)])


def after(array, *done):
    return lax.optimization_barrier((array,) + done)[0]


def per_device(tokens, cotangent, route_ids, route_weights, w_gate, w_up, v_down):
    owners, wide, cores = (lax.axis_size(a) for a in ("expert", "dp", "sub"))
    owner, dp, sub = (lax.axis_index(a) for a in ("expert", "dp", "sub"))
    token_rows, chosen = route_ids.shape
    local_experts = w_gate.shape[0]
    expert_count = owners * local_experts
    most = max(2, 9 * token_rows * chosen // (8 * expert_count))
    quarter = tokens.shape[1] // (wide * cores)
    place = jnp.stack([sub, owner * local_experts, dp]).astype(jnp.int32)

    *sends, own, own_other = pack(
        place, tokens, cotangent, route_ids, route_weights, wide, quarter
    )

    def ahead(mine, other, previous, streamed=False):
        return forward(
            place, mine, other, w_gate, w_up, v_down, token_rows, chosen, most, previous, streamed
        )

    received = [shift(one, "dp", by) for by, one in enumerate(sends, 1)]
    parts = [ahead([own], [own_other], place)]
    blocks, swapped = [[own] + received], [[]]
    for _ in range(1, owners):
        blocks.append([shift(one, "expert", 1) for one in blocks[-1]])
    blocks.append([])
    swapped.append([shift(blocks[1][0], "sub", 1)])
    for one in received:
        other = shift(after(one, parts[0][2]), "sub", 1)
        previous = after(parts[-1][2], swapped[1][0], *blocks[1][1:])
        parts.append(ahead([one], [other], previous))
    home_sums = [[part[0]] for part in parts]
    arrived = []
    for index in range(wide):
        for step in range(1, wide):
            got = shift(parts[index][0], "dp", -step)
            home_sums[(index - step) % wide].append(got)
            arrived.append(got)
    hiddens, cots = [], [part[1] for part in parts]
    waiting = ([part[2] for part in parts], home_sums)
    last = parts[-1][2]
    swapped[1] += [
        shift(after(one, last, *arrived[: wide - 1]), "sub", 1) for one in blocks[1][1:]
    ]
    gate_for_sums = arrived[wide - 1 :]

    def behind(waiting, previous, crossing_after=()):
        hidden, keep, send = backward(place, *waiting, w_gate, w_up, previous)
        hiddens.append(hidden)
        send = after(send, *crossing_after)
        return hidden, (keep, shift(send, "sub", 1))

    direct = wide == cores
    near, far = [], []

    def sent_back(halves, by):
        if by < 2 or not direct:
            (rows,) = small(
                functools.partial(sum_kernel, 2), [halves[0].shape], place, *halves
            )
            near.append(shift(rows, "expert", -by) if by else rows)
            return [rows]
        pieces = small(
            functools.partial(turned_kernel, 2), [(token_rows, quarter)] * 2, place, *halves
        )
        return pieces

    def sent_straight(pieces, by):
        for way, piece in enumerate(pieces):
            pairs = []
            for index in range(owners * wide * cores):
                place_of, from_dp, from_sub = (
                    index // (wide * cores),
                    index // cores % wide,
                    index % cores,
                )
                to = (place_of - by) % owners * wide + (from_sub + way) % wide
                pairs.append((index, to * cores + from_dp))
            far.append(lax.ppermute(piece, ("expert", "dp", "sub"), pairs))

    def gathered(rows):
        pieces = jnp.zeros((wide, token_rows, quarter), BF)
        for by in range(wide):
            one = rows[by * token_rows : (by + 1) * token_rows].astype(BF)
            one = after(shift(one, "dp", -by), last) if by else one
            pieces = lax.dynamic_update_slice_in_dim(pieces, one[None], (dp + by) % wide, 0)
        span = wide // cores
        stay = lax.dynamic_slice_in_dim(pieces, sub * span, span, 0)
        come = shift(lax.dynamic_slice_in_dim(pieces, (1 - sub) * span, span, 0), "sub", 1)
        columns = []
        for index in range(span):
            columns.append(jnp.where(sub == 0, stay[index], come[index]))
            columns.append(jnp.where(sub == 0, come[index], stay[index]))
        return jnp.concatenate(columns, axis=1)

    for by in range(1, owners):
        previous = after(last, *blocks[2][:1]) if by == 1 else last
        sums, cot_rows, tables = ahead(blocks[by], swapped[by], previous)
        cots.append(cot_rows)
        swapped.append([shift(after(one, tables), "sub", 1) for one in blocks[by + 1]])
        send = after(sums, *gate_for_sums, *swapped[by + 1][:1])
        gate_for_sums = [shift(send, "dp", step) for step in range(1, wide)]
        last, halves = behind(waiting, tables, swapped[by + 1])
        pieces = sent_back(halves, by - 1)
        if direct and by - 1 >= 2:
            sent_straight(pieces, by - 1)
        waiting = ([tables], [[sums] + gate_for_sums])
    last, halves = behind(waiting, after(last, *near[-1:], *pieces), far)
    pieces = sent_back(halves, owners - 1)
    if direct and owners > 2:
        hiddens[-1], *pieces = lax.optimization_barrier((last, *pieces))
        sent_straight(pieces, owners - 1)
    grad_down, done = grads(hiddens, cots)
    if not direct or owners < 3:
        return (grad_down, gathered(sum((one.astype(F32) for one in near[1:]), near[0])))
    keep, send = small(
        functools.partial(sum_kernel, len(near)), [(token_rows, quarter)] * 2, place, *near
    )
    got = after(shift(send, "dp", -1), last)
    stay, send = small(choose_kernel, [keep.shape] * 2, place, keep, got)
    come = shift(send, "sub", 1)
    far = [after(one, done) for one in far]
    (out,) = small(
        final_kernel, [(token_rows, cores * quarter)], place, stay, come, *far
    )
    return (grad_down, out)


def solution(mesh):
    placed = (
        P(("groups", "expert", "dp"), None),
        P(("groups", "expert", "dp"), None),
        P(("groups", "expert", "dp"), None),
        P(("groups", "expert", "dp"), None),
        P("expert", "dp", "sub"),
        P("expert", "dp", "sub"),
        P(("groups", "expert"), "sub", "dp"),
    )
    return jax.shard_map(
        per_device,
        mesh=mesh,
        in_specs=placed,
        out_specs=(P(("groups", "expert"), "sub", "dp"), P(("groups", "expert", "dp"), "sub")),
        check_vma=False,
    )
```

```python
import functools

import jax
import jax.numpy as jnp
from jax import lax
from jax.experimental import pallas as pl
from jax.experimental.pallas import tpu as pltpu
from jax.sharding import PartitionSpec as P

BF = jnp.bfloat16
F32 = jnp.float32
LANES = 128


def up_to(value, step):
    return -(-value // step) * step


def dot(a, b, contract=((1,), (0,))):
    return lax.dot_general(a, b, (contract, ((), ())), preferred_element_type=F32)


def vmem_spec(shape):
    return pl.BlockSpec(shape, lambda j: (0,) * len(shape))


def expert_spec(shape):
    return pl.BlockSpec((1,) + shape, lambda j: (j,) + (0,) * len(shape))


def pack_kernel(place, tokens, cotangent, route_ids, route_weights, *refs):
    *outs, ids, weights, sems = refs
    chosen, rows = ids.shape
    quarter = outs[0].shape[1] // 2
    wide = len(outs) - 1
    dp, sub = place[2], place[0]
    copies = [
        pltpu.make_async_copy(route_ids, ids, sems.at[0]),
        pltpu.make_async_copy(route_weights, weights, sems.at[1]),
    ]
    wanted = [((dp + by) % wide, sub) for by in range(1, wide)] + [(dp, sub), (dp, 1 - sub)]
    for out, (half, which) in zip(outs, wanted):
        columns = pl.ds(pl.multiple_of((half * 2 + which) * quarter, LANES), quarter)
        for source, at in ((tokens, 0), (cotangent, quarter)):
            target = out.at[0:rows, at : at + quarter]
            copies.append(
                pltpu.make_async_copy(source.at[:, columns], target, sems.at[len(copies)])
            )
    for copy in copies:
        copy.start()
    copies[0].wait()
    copies[1].wait()
    parts, rest = [ids[...].astype(F32)], weights[...]
    for _ in range(3):
        part = rest.astype(BF).astype(F32)
        parts.append(part)
        rest = rest - part
    table = jnp.concatenate(parts, axis=0)
    per_row = 2 * quarter // rows
    lines = [
        jnp.concatenate([table[i : i + 1] for i in range(start, start + per_row)], axis=1)
        for start in range(0, 4 * chosen, per_row)
    ]
    lines.append(jnp.zeros((ROUTE_ROWS - len(lines), 2 * quarter), F32))
    lines = jnp.concatenate(lines, axis=0).astype(BF)
    for out in outs:
        out[rows:, :] = lines
    for copy in copies[2:]:
        copy.wait()


def pack(place, tokens, cotangent, route_ids, route_weights, wide, quarter):
    rows, chosen = route_ids.shape
    shape = (rows + ROUTE_ROWS, 2 * quarter)
    return pl.pallas_call(
        pack_kernel,
        in_specs=[SMEM] + [pl.BlockSpec(memory_space=pltpu.HBM)] * 4,
        out_specs=[WHOLE] * (wide + 1),
        out_shape=[jax.ShapeDtypeStruct(shape, BF)] * (wide + 1),
        scratch_shapes=[
            pltpu.VMEM((chosen, rows), jnp.int32),
            pltpu.VMEM((chosen, rows), F32),
            pltpu.SemaphoreType.DMA((2 * wide + 4,)),
        ],
        compiler_params=pltpu.CompilerParams(vmem_limit_bytes=LIMIT),
        cost_estimate=PACK_COST,
    )(place, tokens, cotangent, route_ids.T, route_weights.T)


def route_tables(payloads, token_rows, chosen, first_expert, dp, local_experts, tables):
    shards = len(payloads)
    per_row = payloads[0].shape[1] // token_rows
    lines = [payload[token_rows:, :].astype(F32) for payload in payloads]

    def entry(index):
        row, column = divmod(index, per_row)
        at = slice(column * token_rows, (column + 1) * token_rows)
        return jnp.concatenate([line[row : row + 1, at] for line in lines], axis=1)

    ids = [entry(k) for k in range(chosen)]
    weights = [
        entry(chosen + k) + entry(2 * chosen + k) + entry(3 * chosen + k) for k in range(chosen)
    ]
    total = shards * token_rows
    masks, scales = [], []
    for local in range(local_experts):
        wanted = (first_expert + local).astype(F32)
        hits = [(one == wanted).astype(F32) for one in ids]
        masks.append(sum(hits))
        scales.append(sum(hit * weight for hit, weight in zip(hits, weights)))
    pad = [jnp.zeros((8 - local_experts, total), F32)] if local_experts < 8 else []
    mask = jnp.concatenate(masks + pad, axis=0)

    def number(axis):
        index = lax.broadcasted_iota(jnp.int32, (total, total), axis)
        part = sum((index >= i * token_rows).astype(jnp.int32) for i in range(1, shards + 1))
        shard = dp - part
        return index + (jnp.where(shard < 0, shard + shards, shard) - part) * token_rows

    rank = dot(mask.astype(BF), (number(0) < number(1)).astype(F32).astype(BF))
    tables[0:8, :] = jnp.where(mask > 0.5, rank, -1.0)
    tables[8:16, :] = jnp.concatenate(scales + pad, axis=0)


def one_hot(tables, local, slots):
    rank = tables[pl.ds(local, 1), :].astype(jnp.int32)
    total = rank.shape[1]
    return lax.broadcasted_iota(jnp.int32, (slots, total), 0) == rank


def forward_kernel(shards, token_rows, chosen, capacity, streamed, place, *refs):
    mine, other, refs = refs[:shards], refs[shards : 2 * shards], refs[2 * shards :]
    gate, up, down, _, sums, cot_rows, tables, token_scratch, sum_scratch = refs
    quarter = mine[0].shape[1] // 2
    experts = sums.shape[1] // capacity
    slots = cot_rows.shape[1]

    def routing():
        route_tables(mine, token_rows, chosen, place[1], place[2], experts, tables)

    def finish():
        sums[...] = sum_scratch[...].astype(BF)

    def one_expert(local, at):
        hot = one_hot(tables, local, slots).astype(F32).astype(BF)
        for source, which in ((mine, place[0]), (other, 1 - place[0])):
            rows = jnp.concatenate([one[0:token_rows, :] for one in source], axis=0)
            columns = pl.ds(pl.multiple_of(which * quarter, LANES), quarter)
            picked = dot(hot, rows).astype(BF)
            token_scratch[:, columns] = picked[:, :quarter]
            cot_rows[at, :, columns] = picked[:, quarter:]
        start = pl.multiple_of(local * capacity, 8) if streamed else local * capacity
        here = pl.ds(start, capacity)
        sum_scratch[0, here, :] = dot(token_scratch[...], gate[at])[:capacity]
        sum_scratch[1, here, :] = dot(token_scratch[...], up[at])[:capacity]
        sum_scratch[2, here, :] = dot(cot_rows[at], down[at], ((1,), (1,)))[:capacity]

    if streamed:
        local = pl.program_id(0)
        pl.when(local == 0)(routing)
        one_expert(local, 0)
        pl.when(local == experts - 1)(finish)
    else:
        routing()
        for local in range(experts):
            one_expert(local, local)
        finish()


def backward_kernel(capacity, parts, wide, place, *refs):
    tables, refs = refs[:parts], refs[parts:]
    sums, refs = refs[: parts * wide], refs[parts * wide :]
    gate, up, _, hidden, keep, send, full, total = refs
    rows = sums[0].shape[1]
    experts = hidden.shape[0]
    slots = hidden.shape[1] // parts
    quarter = keep.shape[1]
    for part in range(parts):
        here = sums[part * wide : (part + 1) * wide]
        full[part, :, 0:rows, :] = sum(one[...].astype(F32) for one in here)
        full[part, :, rows:, :] = jnp.zeros((3, full.shape[2] - rows, full.shape[3]), F32)
    for local in range(experts):
        gate_tokens, up_tokens = [], []
        for part in range(parts):
            hot = one_hot(tables[part], local, slots).astype(F32)
            scale = jnp.sum(hot * tables[part][8 + local : 9 + local, :], axis=1, keepdims=True)
            here = slice(local * capacity, local * capacity + slots)
            pre_gate, pre_up, tangent = (full[part, i, here, :] for i in range(3))
            sigmoid_gate = jax.nn.sigmoid(pre_gate)
            act = pre_gate * sigmoid_gate
            slope = sigmoid_gate * (1.0 + pre_gate * (1.0 - sigmoid_gate))
            hidden[local, part * slots : (part + 1) * slots, :] = (scale * act * pre_up).astype(BF)
            scaled = scale * tangent
            gate_adjoint = (scaled * pre_up * slope).astype(BF)
            up_adjoint = (scaled * act).astype(BF)
            hot = hot.astype(BF)
            gate_tokens.append(dot(hot, gate_adjoint, ((0,), (0,))).astype(BF))
            up_tokens.append(dot(hot, up_adjoint, ((0,), (0,))).astype(BF))
        gate_tokens = jnp.concatenate(gate_tokens, axis=0)
        up_tokens = jnp.concatenate(up_tokens, axis=0)
        term = dot(gate_tokens, gate[local], ((1,), (1,)))
        term = term + dot(up_tokens, up[local], ((1,), (1,)))
        total[...] = term if local == 0 else total[...] + term
    for out, which in ((keep, place[0]), (send, 1 - place[0])):
        out[...] = total[:, pl.ds(pl.multiple_of(which * quarter, LANES), quarter)].astype(BF)


def grad_kernel(half, *refs):
    *inputs, out, done = refs
    done[...] = jnp.zeros_like(done)
    local = pl.program_id(0)
    hidden = jnp.concatenate([one[local] for one in inputs[:half]], axis=0)
    cot_rows = jnp.concatenate([one[local] for one in inputs[half:]], axis=0)
    out[0] = dot(hidden, cot_rows, ((0,), (0,))).astype(BF)


SMEM = pl.BlockSpec(memory_space=pltpu.SMEM)
ANY = pl.BlockSpec(memory_space=pl.ANY)
WHOLE = pl.BlockSpec(memory_space=pltpu.VMEM)
LIMIT = 12 * 1024 * 1024
STREAM_LIMIT = 60 * 1024 * 1024
ROUTE_ROWS = 16
PACK_COST = pl.CostEstimate(flops=1, bytes_accessed=32 * 1024 * 1024, transcendentals=0)
NO_COST = pl.CostEstimate(flops=1, bytes_accessed=1, transcendentals=0)


def forward(
    place, mine, other, gate, up, down, token_rows, chosen, most, previous, streamed=False
):
    local_experts, depth, hidden = gate.shape
    shards = len(mine)
    capacity = up_to(shards * most, 8)
    slots = up_to(capacity, 16)
    rows = local_experts * capacity
    tokens = shards * token_rows
    weights = [WHOLE] * 3
    if streamed:
        weights = [expert_spec((depth, hidden))] * 2 + [expert_spec((hidden, depth))]
    return pl.pallas_call(
        functools.partial(forward_kernel, shards, token_rows, chosen, capacity, streamed),
        grid=(local_experts,) if streamed else (),
        in_specs=[SMEM] + [WHOLE] * (2 * shards) + weights + [ANY],
        out_specs=[WHOLE, expert_spec((slots, depth)) if streamed else WHOLE, WHOLE],
        out_shape=[
            jax.ShapeDtypeStruct((3, rows, hidden), BF),
            jax.ShapeDtypeStruct((local_experts, slots, depth), BF),
            jax.ShapeDtypeStruct((16, tokens), F32),
        ],
        scratch_shapes=[pltpu.VMEM((slots, depth), BF), pltpu.VMEM((3, rows, hidden), F32)],
        compiler_params=pltpu.CompilerParams(vmem_limit_bytes=STREAM_LIMIT if streamed else LIMIT),
        cost_estimate=NO_COST,
    )(place, *mine, *other, gate, up, down, previous)


def backward(place, tables, sums, gate, up, previous):
    local_experts, depth, hidden = gate.shape
    parts, wide = len(tables), len(sums[0])
    rows = sums[0][0].shape[1]
    capacity = rows // local_experts
    slots = up_to(capacity, 16)
    tokens = parts * tables[0].shape[1]
    flat = [one for part in sums for one in part]
    return pl.pallas_call(
        functools.partial(backward_kernel, capacity, parts, wide),
        in_specs=[SMEM] + [WHOLE] * (parts + len(flat) + 2) + [ANY],
        out_specs=[WHOLE] * 3,
        out_shape=[
            jax.ShapeDtypeStruct((local_experts, parts * slots, hidden), BF),
            jax.ShapeDtypeStruct((tokens, depth // 2), BF),
            jax.ShapeDtypeStruct((tokens, depth // 2), BF),
        ],
        scratch_shapes=[
            pltpu.VMEM((parts, 3, rows + slots - capacity + 8, hidden), F32),
            pltpu.VMEM((tokens, depth), F32),
        ],
        compiler_params=pltpu.CompilerParams(vmem_limit_bytes=LIMIT),
        cost_estimate=NO_COST,
    )(place, *tables, *flat, gate, up, previous)


def grads(hiddens, cots):
    local_experts, _, hidden = hiddens[0].shape
    depth = cots[0].shape[2]
    slots = sum(one.shape[1] for one in cots)
    return pl.pallas_call(
        functools.partial(grad_kernel, len(hiddens)),
        grid=(local_experts,),
        in_specs=[WHOLE] * (len(hiddens) + len(cots)),
        out_specs=[expert_spec((hidden, depth)), vmem_spec((8, LANES))],
        out_shape=[
            jax.ShapeDtypeStruct((local_experts, hidden, depth), BF),
            jax.ShapeDtypeStruct((8, LANES), F32),
        ],
        compiler_params=pltpu.CompilerParams(vmem_limit_bytes=LIMIT),
        cost_estimate=NO_COST,
    )(*hiddens, *cots)


def small(kernel, shapes, *arrays):
    return pl.pallas_call(
        kernel,
        in_specs=[SMEM] + [WHOLE] * (len(arrays) - 1),
        out_specs=[WHOLE] * len(shapes),
        out_shape=[jax.ShapeDtypeStruct(shape, BF) for shape in shapes],
        compiler_params=pltpu.CompilerParams(vmem_limit_bytes=LIMIT),
        cost_estimate=NO_COST,
    )(*arrays)


def sum_kernel(inputs, place, *refs):
    total = sum(one[...].astype(F32) for one in refs[:inputs]).astype(BF)
    rows = refs[inputs].shape[0]
    for index, out in enumerate(refs[inputs:]):
        out[...] = total[index * rows : (index + 1) * rows]


def turned_kernel(inputs, place, *refs):
    total = sum(one[...].astype(F32) for one in refs[:inputs]).astype(BF)
    first, second = refs[inputs:]
    rows = first.shape[0]
    straight = place[2] == place[0]

    @pl.when(straight)
    def _():
        first[...] = total[:rows]
        second[...] = total[rows:]

    @pl.when(jnp.logical_not(straight))
    def _():
        first[...] = total[rows:]
        second[...] = total[:rows]


def choose_kernel(place, one, two, stay, send):
    straight = place[2] == place[0]

    @pl.when(straight)
    def _():
        stay[...] = one[...]
        send[...] = two[...]

    @pl.when(jnp.logical_not(straight))
    def _():
        stay[...] = two[...]
        send[...] = one[...]


def final_kernel(place, stay, come, *refs):
    *far, out = refs
    quarter = stay.shape[1]

    def far_sum(flip):
        return [
            sum(far[start + (q + flip) % 2][...].astype(F32) for start in range(0, len(far), 2))
            for q in range(2)
        ]

    for sub in range(2):
        for dp in range(2):

            @pl.when((place[0] == sub) & (place[2] == dp))
            def _():
                own = [stay[...], come[...]] if sub == 0 else [come[...], stay[...]]
                for q, extra in enumerate(far_sum(dp)):
                    out[:, q * quarter : (q + 1) * quarter] = (own[q].astype(F32) + extra).astype(BF)


def shift(array, axis, by):
    size = lax.axis_size(axis)
    return lax.ppermute(array, axis, [(i, (i + by) % size) for i in range(size)])


def after(array, *done):
    return lax.optimization_barrier((array,) + done)[0]


def per_device(tokens, cotangent, route_ids, route_weights, w_gate, w_up, v_down):
    owners, wide, cores = (lax.axis_size(a) for a in ("expert", "dp", "sub"))
    owner, dp, sub = (lax.axis_index(a) for a in ("expert", "dp", "sub"))
    token_rows, chosen = route_ids.shape
    local_experts = w_gate.shape[0]
    expert_count = owners * local_experts
    most = max(2, 9 * token_rows * chosen // (8 * expert_count))
    quarter = tokens.shape[1] // (wide * cores)
    place = jnp.stack([sub, owner * local_experts, dp]).astype(jnp.int32)

    *sends, own, own_other = pack(
        place, tokens, cotangent, route_ids, route_weights, wide, quarter
    )

    def ahead(mine, other, previous, streamed=False):
        return forward(
            place, mine, other, w_gate, w_up, v_down, token_rows, chosen, most, previous, streamed
        )

    received = [shift(one, "dp", by) for by, one in enumerate(sends, 1)]
    parts = [ahead([own], [own_other], place)]
    blocks, swapped = [[own] + received], [[]]
    for _ in range(1, owners):
        blocks.append([shift(one, "expert", 1) for one in blocks[-1]])
    blocks.append([])
    swapped.append([shift(blocks[1][0], "sub", 1)])
    for one in received:
        other = shift(after(one, parts[0][2]), "sub", 1)
        previous = after(parts[-1][2], swapped[1][0])
        parts.append(ahead([one], [other], previous))
    home_sums = [[part[0]] for part in parts]
    arrived = []
    for index in range(wide):
        for step in range(1, wide):
            got = shift(parts[index][0], "dp", -step)
            home_sums[(index - step) % wide].append(got)
            arrived.append(got)
    hiddens, cots = [], [part[1] for part in parts]
    waiting = ([part[2] for part in parts], home_sums)
    last = parts[-1][2]
    swapped[1] += [
        shift(after(one, last, *arrived[: wide - 1]), "sub", 1) for one in blocks[1][1:]
    ]
    gate_for_sums = arrived[wide - 1 :]

    def behind(waiting, previous, crossing_after=()):
        hidden, keep, send = backward(place, *waiting, w_gate, w_up, previous)
        hiddens.append(hidden)
        send = after(send, *crossing_after)
        return hidden, (keep, shift(send, "sub", 1))

    direct = wide == cores
    near, far = [], []

    def sent_back(halves, by):
        if by < 2 or not direct:
            (rows,) = small(
                functools.partial(sum_kernel, 2), [halves[0].shape], place, *halves
            )
            near.append(shift(rows, "expert", -by) if by else rows)
            return [rows]
        pieces = small(
            functools.partial(turned_kernel, 2), [(token_rows, quarter)] * 2, place, *halves
        )
        return pieces

    def sent_straight(pieces, by):
        for way, piece in enumerate(pieces):
            pairs = []
            for index in range(owners * wide * cores):
                place_of, from_dp, from_sub = (
                    index // (wide * cores),
                    index // cores % wide,
                    index % cores,
                )
                to = (place_of - by) % owners * wide + (from_sub + way) % wide
                pairs.append((index, to * cores + from_dp))
            far.append(lax.ppermute(piece, ("expert", "dp", "sub"), pairs))

    def gathered(rows):
        pieces = jnp.zeros((wide, token_rows, quarter), BF)
        for by in range(wide):
            one = rows[by * token_rows : (by + 1) * token_rows].astype(BF)
            one = after(shift(one, "dp", -by), last) if by else one
            pieces = lax.dynamic_update_slice_in_dim(pieces, one[None], (dp + by) % wide, 0)
        span = wide // cores
        stay = lax.dynamic_slice_in_dim(pieces, sub * span, span, 0)
        come = shift(lax.dynamic_slice_in_dim(pieces, (1 - sub) * span, span, 0), "sub", 1)
        columns = []
        for index in range(span):
            columns.append(jnp.where(sub == 0, stay[index], come[index]))
            columns.append(jnp.where(sub == 0, come[index], stay[index]))
        return jnp.concatenate(columns, axis=1)

    for by in range(1, owners):
        sums, cot_rows, tables = ahead(blocks[by], swapped[by], last)
        cots.append(cot_rows)
        send = after(sums, *gate_for_sums)
        gate_for_sums = [shift(send, "dp", step) for step in range(1, wide)]
        last, halves = behind(waiting, tables)
        pieces = sent_back(halves, by - 1)
        if direct and by - 1 >= 2:
            sent_straight(pieces, by - 1)
        waiting = ([tables], [[sums] + gate_for_sums])
        swapped.append([])
        for one in blocks[by + 1]:
            one = after(one, last, *blocks[by + 1], *swapped[-1])
            swapped[-1].append(shift(one, "sub", 1))
    if not direct or owners < 3:
        last, halves = behind(waiting, after(last, *pieces))
        sent_back(halves, owners - 1)
        grad_down, _ = grads(hiddens, cots)
        return (grad_down, gathered(sum((one.astype(F32) for one in near[1:]), near[0])))
    last, halves = behind(waiting, after(last, *pieces), far)
    pieces = sent_back(halves, owners - 1)
    keep, send = small(
        functools.partial(sum_kernel, len(near)), [(token_rows, quarter)] * 2, place,
        *near[:-1], after(near[-1], last),
    )
    got = shift(send, "dp", -1)
    hiddens[-1], *pieces = lax.optimization_barrier((last, *pieces))
    sent_straight(pieces, owners - 1)
    grad_down, done = grads(hiddens, cots)
    stay, send = small(choose_kernel, [keep.shape] * 2, place, keep, got)
    come = shift(send, "sub", 1)
    far = [after(one, done) for one in far]
    (out,) = small(
        final_kernel, [(token_rows, cores * quarter)], place, stay, come, *far
    )
    return (grad_down, out)


def solution(mesh):
    placed = (
        P(("groups", "expert", "dp"), None),
        P(("groups", "expert", "dp"), None),
        P(("groups", "expert", "dp"), None),
        P(("groups", "expert", "dp"), None),
        P("expert", "dp", "sub"),
        P("expert", "dp", "sub"),
        P(("groups", "expert"), "sub", "dp"),
    )
    return jax.shard_map(
        per_device,
        mesh=mesh,
        in_specs=placed,
        out_specs=(P(("groups", "expert"), "sub", "dp"), P(("groups", "expert", "dp"), "sub")),
        check_vma=False,
    )
```

```python
import functools

import jax
import jax.numpy as jnp
from jax import lax
from jax.experimental import pallas as pl
from jax.experimental.pallas import tpu as pltpu
from jax.sharding import PartitionSpec as P

BF = jnp.bfloat16
F32 = jnp.float32
LANES = 128


def up_to(value, step):
    return -(-value // step) * step


def dot(a, b, contract=((1,), (0,))):
    return lax.dot_general(a, b, (contract, ((), ())), preferred_element_type=F32)


def vmem_spec(shape):
    return pl.BlockSpec(shape, lambda j: (0,) * len(shape))


def expert_spec(shape):
    return pl.BlockSpec((1,) + shape, lambda j: (j,) + (0,) * len(shape))


def pack_kernel(place, tokens, cotangent, route_ids, route_weights, *refs):
    *outs, ids, weights, sems = refs
    chosen, rows = ids.shape
    quarter = outs[0].shape[1] // 2
    wide = len(outs) - 1
    dp, sub = place[2], place[0]
    copies = [
        pltpu.make_async_copy(route_ids, ids, sems.at[0]),
        pltpu.make_async_copy(route_weights, weights, sems.at[1]),
    ]
    wanted = [((dp + by) % wide, sub) for by in range(1, wide)] + [(dp, sub), (dp, 1 - sub)]
    for out, (half, which) in zip(outs, wanted):
        columns = pl.ds(pl.multiple_of((half * 2 + which) * quarter, LANES), quarter)
        for source, at in ((tokens, 0), (cotangent, quarter)):
            target = out.at[0:rows, at : at + quarter]
            copies.append(
                pltpu.make_async_copy(source.at[:, columns], target, sems.at[len(copies)])
            )
    for copy in copies:
        copy.start()
    copies[0].wait()
    copies[1].wait()
    parts, rest = [ids[...].astype(F32)], weights[...]
    for _ in range(3):
        part = rest.astype(BF).astype(F32)
        parts.append(part)
        rest = rest - part
    table = jnp.concatenate(parts, axis=0)
    per_row = 2 * quarter // rows
    lines = [
        jnp.concatenate([table[i : i + 1] for i in range(start, start + per_row)], axis=1)
        for start in range(0, 4 * chosen, per_row)
    ]
    lines.append(jnp.zeros((ROUTE_ROWS - len(lines), 2 * quarter), F32))
    lines = jnp.concatenate(lines, axis=0).astype(BF)
    for out in outs:
        out[rows:, :] = lines
    for copy in copies[2:]:
        copy.wait()


def pack(place, tokens, cotangent, route_ids, route_weights, wide, quarter):
    rows, chosen = route_ids.shape
    shape = (rows + ROUTE_ROWS, 2 * quarter)
    return pl.pallas_call(
        pack_kernel,
        in_specs=[SMEM] + [pl.BlockSpec(memory_space=pltpu.HBM)] * 4,
        out_specs=[WHOLE] * (wide + 1),
        out_shape=[jax.ShapeDtypeStruct(shape, BF)] * (wide + 1),
        scratch_shapes=[
            pltpu.VMEM((chosen, rows), jnp.int32),
            pltpu.VMEM((chosen, rows), F32),
            pltpu.SemaphoreType.DMA((2 * wide + 4,)),
        ],
        compiler_params=pltpu.CompilerParams(vmem_limit_bytes=LIMIT),
        cost_estimate=PACK_COST,
    )(place, tokens, cotangent, route_ids.T, route_weights.T)


def route_tables(payloads, token_rows, chosen, first_expert, dp, local_experts, tables):
    shards = len(payloads)
    per_row = payloads[0].shape[1] // token_rows
    lines = [payload[token_rows:, :].astype(F32) for payload in payloads]

    def entry(index):
        row, column = divmod(index, per_row)
        at = slice(column * token_rows, (column + 1) * token_rows)
        return jnp.concatenate([line[row : row + 1, at] for line in lines], axis=1)

    ids = [entry(k) for k in range(chosen)]
    weights = [
        entry(chosen + k) + entry(2 * chosen + k) + entry(3 * chosen + k) for k in range(chosen)
    ]
    total = shards * token_rows
    masks, scales = [], []
    for local in range(local_experts):
        wanted = (first_expert + local).astype(F32)
        hits = [(one == wanted).astype(F32) for one in ids]
        masks.append(sum(hits))
        scales.append(sum(hit * weight for hit, weight in zip(hits, weights)))
    pad = [jnp.zeros((8 - local_experts, total), F32)] if local_experts < 8 else []
    mask = jnp.concatenate(masks + pad, axis=0)

    def number(axis):
        index = lax.broadcasted_iota(jnp.int32, (total, total), axis)
        part = sum((index >= i * token_rows).astype(jnp.int32) for i in range(1, shards + 1))
        shard = dp - part
        return index + (jnp.where(shard < 0, shard + shards, shard) - part) * token_rows

    rank = dot(mask.astype(BF), (number(0) < number(1)).astype(F32).astype(BF))
    tables[0:8, :] = jnp.where(mask > 0.5, rank, -1.0)
    tables[8:16, :] = jnp.concatenate(scales + pad, axis=0)


def one_hot(tables, local, slots):
    rank = tables[pl.ds(local, 1), :].astype(jnp.int32)
    total = rank.shape[1]
    return lax.broadcasted_iota(jnp.int32, (slots, total), 0) == rank


def forward_kernel(shards, token_rows, chosen, capacity, streamed, place, *refs):
    mine, other, refs = refs[:shards], refs[shards : 2 * shards], refs[2 * shards :]
    gate, up, down, _, sums, cot_rows, tables, token_scratch, sum_scratch = refs
    quarter = mine[0].shape[1] // 2
    experts = sums.shape[1] // capacity
    slots = cot_rows.shape[1]

    def routing():
        route_tables(mine, token_rows, chosen, place[1], place[2], experts, tables)

    def finish():
        sums[...] = sum_scratch[...].astype(BF)

    def one_expert(local, at):
        hot = one_hot(tables, local, slots).astype(F32).astype(BF)
        for source, which in ((mine, place[0]), (other, 1 - place[0])):
            rows = jnp.concatenate([one[0:token_rows, :] for one in source], axis=0)
            columns = pl.ds(pl.multiple_of(which * quarter, LANES), quarter)
            picked = dot(hot, rows).astype(BF)
            token_scratch[:, columns] = picked[:, :quarter]
            cot_rows[at, :, columns] = picked[:, quarter:]
        start = pl.multiple_of(local * capacity, 8) if streamed else local * capacity
        here = pl.ds(start, capacity)
        sum_scratch[0, here, :] = dot(token_scratch[...], gate[at])[:capacity]
        sum_scratch[1, here, :] = dot(token_scratch[...], up[at])[:capacity]
        sum_scratch[2, here, :] = dot(cot_rows[at], down[at], ((1,), (1,)))[:capacity]

    if streamed:
        local = pl.program_id(0)
        pl.when(local == 0)(routing)
        one_expert(local, 0)
        pl.when(local == experts - 1)(finish)
    else:
        routing()
        for local in range(experts):
            one_expert(local, local)
        finish()


def backward_kernel(capacity, parts, wide, place, *refs):
    tables, refs = refs[:parts], refs[parts:]
    sums, refs = refs[: parts * wide], refs[parts * wide :]
    gate, up, _, hidden, keep, send, full, total = refs
    rows = sums[0].shape[1]
    experts = hidden.shape[0]
    slots = hidden.shape[1] // parts
    quarter = keep.shape[1]
    for part in range(parts):
        here = sums[part * wide : (part + 1) * wide]
        full[part, :, 0:rows, :] = sum(one[...].astype(F32) for one in here)
        full[part, :, rows:, :] = jnp.zeros((3, full.shape[2] - rows, full.shape[3]), F32)
    for local in range(experts):
        gate_tokens, up_tokens = [], []
        for part in range(parts):
            hot = one_hot(tables[part], local, slots).astype(F32)
            scale = jnp.sum(hot * tables[part][8 + local : 9 + local, :], axis=1, keepdims=True)
            here = slice(local * capacity, local * capacity + slots)
            pre_gate, pre_up, tangent = (full[part, i, here, :] for i in range(3))
            sigmoid_gate = jax.nn.sigmoid(pre_gate)
            act = pre_gate * sigmoid_gate
            slope = sigmoid_gate * (1.0 + pre_gate * (1.0 - sigmoid_gate))
            hidden[local, part * slots : (part + 1) * slots, :] = (scale * act * pre_up).astype(BF)
            scaled = scale * tangent
            gate_adjoint = (scaled * pre_up * slope).astype(BF)
            up_adjoint = (scaled * act).astype(BF)
            hot = hot.astype(BF)
            gate_tokens.append(dot(hot, gate_adjoint, ((0,), (0,))).astype(BF))
            up_tokens.append(dot(hot, up_adjoint, ((0,), (0,))).astype(BF))
        gate_tokens = jnp.concatenate(gate_tokens, axis=0)
        up_tokens = jnp.concatenate(up_tokens, axis=0)
        term = dot(gate_tokens, gate[local], ((1,), (1,)))
        term = term + dot(up_tokens, up[local], ((1,), (1,)))
        total[...] = term if local == 0 else total[...] + term
    for out, which in ((keep, place[0]), (send, 1 - place[0])):
        out[...] = total[:, pl.ds(pl.multiple_of(which * quarter, LANES), quarter)].astype(BF)


def grad_kernel(half, *refs):
    *inputs, out, done = refs
    done[...] = jnp.zeros_like(done)
    local = pl.program_id(0)
    hidden = jnp.concatenate([one[local] for one in inputs[:half]], axis=0)
    cot_rows = jnp.concatenate([one[local] for one in inputs[half:]], axis=0)
    out[0] = dot(hidden, cot_rows, ((0,), (0,))).astype(BF)


SMEM = pl.BlockSpec(memory_space=pltpu.SMEM)
ANY = pl.BlockSpec(memory_space=pl.ANY)
WHOLE = pl.BlockSpec(memory_space=pltpu.VMEM)
LIMIT = 12 * 1024 * 1024
STREAM_LIMIT = 60 * 1024 * 1024
ROUTE_ROWS = 16
PACK_COST = pl.CostEstimate(flops=1, bytes_accessed=32 * 1024 * 1024, transcendentals=0)
NO_COST = pl.CostEstimate(flops=1, bytes_accessed=1, transcendentals=0)


def forward(
    place, mine, other, gate, up, down, token_rows, chosen, most, previous, streamed=False
):
    local_experts, depth, hidden = gate.shape
    shards = len(mine)
    capacity = up_to(shards * most, 8)
    slots = up_to(capacity, 16)
    rows = local_experts * capacity
    tokens = shards * token_rows
    weights = [WHOLE] * 3
    if streamed:
        weights = [expert_spec((depth, hidden))] * 2 + [expert_spec((hidden, depth))]
    return pl.pallas_call(
        functools.partial(forward_kernel, shards, token_rows, chosen, capacity, streamed),
        grid=(local_experts,) if streamed else (),
        in_specs=[SMEM] + [WHOLE] * (2 * shards) + weights + [ANY],
        out_specs=[WHOLE, expert_spec((slots, depth)) if streamed else WHOLE, WHOLE],
        out_shape=[
            jax.ShapeDtypeStruct((3, rows, hidden), BF),
            jax.ShapeDtypeStruct((local_experts, slots, depth), BF),
            jax.ShapeDtypeStruct((16, tokens), F32),
        ],
        scratch_shapes=[pltpu.VMEM((slots, depth), BF), pltpu.VMEM((3, rows, hidden), F32)],
        compiler_params=pltpu.CompilerParams(vmem_limit_bytes=STREAM_LIMIT if streamed else LIMIT),
        cost_estimate=NO_COST,
    )(place, *mine, *other, gate, up, down, previous)


def backward(place, tables, sums, gate, up, previous):
    local_experts, depth, hidden = gate.shape
    parts, wide = len(tables), len(sums[0])
    rows = sums[0][0].shape[1]
    capacity = rows // local_experts
    slots = up_to(capacity, 16)
    tokens = parts * tables[0].shape[1]
    flat = [one for part in sums for one in part]
    return pl.pallas_call(
        functools.partial(backward_kernel, capacity, parts, wide),
        in_specs=[SMEM] + [WHOLE] * (parts + len(flat) + 2) + [ANY],
        out_specs=[WHOLE] * 3,
        out_shape=[
            jax.ShapeDtypeStruct((local_experts, parts * slots, hidden), BF),
            jax.ShapeDtypeStruct((tokens, depth // 2), BF),
            jax.ShapeDtypeStruct((tokens, depth // 2), BF),
        ],
        scratch_shapes=[
            pltpu.VMEM((parts, 3, rows + slots - capacity + 8, hidden), F32),
            pltpu.VMEM((tokens, depth), F32),
        ],
        compiler_params=pltpu.CompilerParams(vmem_limit_bytes=LIMIT),
        cost_estimate=NO_COST,
    )(place, *tables, *flat, gate, up, previous)


def grads(hiddens, cots):
    local_experts, _, hidden = hiddens[0].shape
    depth = cots[0].shape[2]
    slots = sum(one.shape[1] for one in cots)
    return pl.pallas_call(
        functools.partial(grad_kernel, len(hiddens)),
        grid=(local_experts,),
        in_specs=[WHOLE] * (len(hiddens) + len(cots)),
        out_specs=[expert_spec((hidden, depth)), vmem_spec((8, LANES))],
        out_shape=[
            jax.ShapeDtypeStruct((local_experts, hidden, depth), BF),
            jax.ShapeDtypeStruct((8, LANES), F32),
        ],
        compiler_params=pltpu.CompilerParams(vmem_limit_bytes=LIMIT),
        cost_estimate=NO_COST,
    )(*hiddens, *cots)


def small(kernel, shapes, *arrays):
    return pl.pallas_call(
        kernel,
        in_specs=[SMEM] + [WHOLE] * (len(arrays) - 1),
        out_specs=[WHOLE] * len(shapes),
        out_shape=[jax.ShapeDtypeStruct(shape, BF) for shape in shapes],
        compiler_params=pltpu.CompilerParams(vmem_limit_bytes=LIMIT),
        cost_estimate=NO_COST,
    )(*arrays)


def sum_kernel(inputs, place, *refs):
    total = sum(one[...].astype(F32) for one in refs[:inputs]).astype(BF)
    rows = refs[inputs].shape[0]
    for index, out in enumerate(refs[inputs:]):
        out[...] = total[index * rows : (index + 1) * rows]


def turned_kernel(inputs, place, *refs):
    total = sum(one[...].astype(F32) for one in refs[:inputs]).astype(BF)
    first, second = refs[inputs:]
    rows = first.shape[0]
    straight = place[2] == place[0]

    @pl.when(straight)
    def _():
        first[...] = total[:rows]
        second[...] = total[rows:]

    @pl.when(jnp.logical_not(straight))
    def _():
        first[...] = total[rows:]
        second[...] = total[:rows]


def choose_kernel(place, one, two, stay, send):
    straight = place[2] == place[0]

    @pl.when(straight)
    def _():
        stay[...] = one[...]
        send[...] = two[...]

    @pl.when(jnp.logical_not(straight))
    def _():
        stay[...] = two[...]
        send[...] = one[...]


def final_kernel(place, stay, come, *refs):
    *far, out = refs
    quarter = stay.shape[1]

    def far_sum(flip):
        return [
            sum(far[start + (q + flip) % 2][...].astype(F32) for start in range(0, len(far), 2))
            for q in range(2)
        ]

    for sub in range(2):
        for dp in range(2):

            @pl.when((place[0] == sub) & (place[2] == dp))
            def _():
                own = [stay[...], come[...]] if sub == 0 else [come[...], stay[...]]
                for q, extra in enumerate(far_sum(dp)):
                    out[:, q * quarter : (q + 1) * quarter] = (own[q].astype(F32) + extra).astype(BF)


def shift(array, axis, by):
    size = lax.axis_size(axis)
    return lax.ppermute(array, axis, [(i, (i + by) % size) for i in range(size)])


def after(array, *done):
    return lax.optimization_barrier((array,) + done)[0]


def per_device(tokens, cotangent, route_ids, route_weights, w_gate, w_up, v_down):
    owners, wide, cores = (lax.axis_size(a) for a in ("expert", "dp", "sub"))
    owner, dp, sub = (lax.axis_index(a) for a in ("expert", "dp", "sub"))
    token_rows, chosen = route_ids.shape
    local_experts = w_gate.shape[0]
    expert_count = owners * local_experts
    most = max(2, 9 * token_rows * chosen // (8 * expert_count))
    quarter = tokens.shape[1] // (wide * cores)
    place = jnp.stack([sub, owner * local_experts, dp]).astype(jnp.int32)

    *sends, own, own_other = pack(
        place, tokens, cotangent, route_ids, route_weights, wide, quarter
    )

    def ahead(mine, other, previous, streamed=False):
        return forward(
            place, mine, other, w_gate, w_up, v_down, token_rows, chosen, most, previous, streamed
        )

    received = [shift(one, "dp", by) for by, one in enumerate(sends, 1)]
    parts = [ahead([own], [own_other], place)]
    blocks, swapped = [[own] + received], [[]]
    for by in range(1, owners):
        blocks.append([])
        for one in blocks[-2]:
            one = after(one, *blocks[-1]) if by == 2 else one
            blocks[-1].append(shift(one, "expert", 1))
    blocks.append([])
    swapped.append([shift(blocks[1][0], "sub", 1)])
    for one in received:
        other = shift(after(one, parts[0][2]), "sub", 1)
        previous = after(parts[-1][2], swapped[1][0])
        parts.append(ahead([one], [other], previous))
    home_sums = [[part[0]] for part in parts]
    arrived = []
    for index in range(wide):
        for step in range(1, wide):
            got = shift(parts[index][0], "dp", -step)
            home_sums[(index - step) % wide].append(got)
            arrived.append(got)
    hiddens, cots = [], [part[1] for part in parts]
    waiting = ([part[2] for part in parts], home_sums)
    last = parts[-1][2]
    swapped[1] += [
        shift(after(one, last, *arrived[: wide - 1]), "sub", 1) for one in blocks[1][1:]
    ]
    gate_for_sums = arrived[wide - 1 :]

    def behind(waiting, previous, crossing_after=()):
        hidden, keep, send = backward(place, *waiting, w_gate, w_up, previous)
        hiddens.append(hidden)
        send = after(send, *crossing_after)
        return hidden, (keep, shift(send, "sub", 1))

    direct = wide == cores
    near, far = [], []

    def sent_back(halves, by):
        if by < 2 or not direct:
            (rows,) = small(
                functools.partial(sum_kernel, 2), [halves[0].shape], place, *halves
            )
            near.append(shift(rows, "expert", -by) if by else rows)
            return [rows]
        pieces = small(
            functools.partial(turned_kernel, 2), [(token_rows, quarter)] * 2, place, *halves
        )
        return pieces

    def sent_straight(pieces, by):
        for way, piece in enumerate(pieces):
            pairs = []
            for index in range(owners * wide * cores):
                place_of, from_dp, from_sub = (
                    index // (wide * cores),
                    index // cores % wide,
                    index % cores,
                )
                to = (place_of - by) % owners * wide + (from_sub + way) % wide
                pairs.append((index, to * cores + from_dp))
            far.append(lax.ppermute(piece, ("expert", "dp", "sub"), pairs))

    def gathered(rows):
        pieces = jnp.zeros((wide, token_rows, quarter), BF)
        for by in range(wide):
            one = rows[by * token_rows : (by + 1) * token_rows].astype(BF)
            one = after(shift(one, "dp", -by), last) if by else one
            pieces = lax.dynamic_update_slice_in_dim(pieces, one[None], (dp + by) % wide, 0)
        span = wide // cores
        stay = lax.dynamic_slice_in_dim(pieces, sub * span, span, 0)
        come = shift(lax.dynamic_slice_in_dim(pieces, (1 - sub) * span, span, 0), "sub", 1)
        columns = []
        for index in range(span):
            columns.append(jnp.where(sub == 0, stay[index], come[index]))
            columns.append(jnp.where(sub == 0, come[index], stay[index]))
        return jnp.concatenate(columns, axis=1)

    for by in range(1, owners):
        sums, cot_rows, tables = ahead(blocks[by], swapped[by], last)
        cots.append(cot_rows)
        send = after(sums, *gate_for_sums)
        gate_for_sums = [shift(send, "dp", step) for step in range(1, wide)]
        last, halves = behind(waiting, tables)
        pieces = sent_back(halves, by - 1)
        if direct and by - 1 >= 2:
            sent_straight(pieces, by - 1)
        waiting = ([tables], [[sums] + gate_for_sums])
        swapped.append([])
        for one in blocks[by + 1]:
            one = after(one, last, *blocks[by + 1], *swapped[-1])
            swapped[-1].append(shift(one, "sub", 1))
    if not direct or owners < 3:
        last, halves = behind(waiting, after(last, *pieces))
        sent_back(halves, owners - 1)
        grad_down, _ = grads(hiddens, cots)
        return (grad_down, gathered(sum((one.astype(F32) for one in near[1:]), near[0])))
    last, halves = behind(waiting, after(last, *pieces), far)
    pieces = sent_back(halves, owners - 1)
    keep, send = small(
        functools.partial(sum_kernel, len(near)), [(token_rows, quarter)] * 2, place,
        *near[:-1], after(near[-1], last),
    )
    got = shift(send, "dp", -1)
    hiddens[-1], *pieces = lax.optimization_barrier((last, *pieces))
    sent_straight(pieces, owners - 1)
    grad_down, done = grads(hiddens, cots)
    stay, send = small(choose_kernel, [keep.shape] * 2, place, keep, got)
    come = shift(send, "sub", 1)
    far = [after(one, done) for one in far]
    (out,) = small(
        final_kernel, [(token_rows, cores * quarter)], place, stay, come, *far
    )
    return (grad_down, out)


def solution(mesh):
    placed = (
        P(("groups", "expert", "dp"), None),
        P(("groups", "expert", "dp"), None),
        P(("groups", "expert", "dp"), None),
        P(("groups", "expert", "dp"), None),
        P("expert", "dp", "sub"),
        P("expert", "dp", "sub"),
        P(("groups", "expert"), "sub", "dp"),
    )
    return jax.shard_map(
        per_device,
        mesh=mesh,
        in_specs=placed,
        out_specs=(P(("groups", "expert"), "sub", "dp"), P(("groups", "expert", "dp"), "sub")),
        check_vma=False,
    )
```

```python
import functools

import jax
import jax.numpy as jnp
from jax import lax
from jax.experimental import pallas as pl
from jax.experimental.pallas import tpu as pltpu
from jax.sharding import PartitionSpec as P

BF = jnp.bfloat16
F32 = jnp.float32
LANES = 128


def up_to(value, step):
    return -(-value // step) * step


def dot(a, b, contract=((1,), (0,))):
    return lax.dot_general(a, b, (contract, ((), ())), preferred_element_type=F32)


def vmem_spec(shape):
    return pl.BlockSpec(shape, lambda j: (0,) * len(shape))


def expert_spec(shape):
    return pl.BlockSpec((1,) + shape, lambda j: (j,) + (0,) * len(shape))


def pack_kernel(place, tokens, cotangent, routes, *refs):
    *outs, sems = refs
    chosen, rows = routes.shape[0] // 2, routes.shape[1]
    quarter = outs[0].shape[1] // 2
    wide = len(outs) - 1
    dp, sub = place[2], place[0]
    copies = []
    wanted = [((dp + by) % wide, sub) for by in range(1, wide)] + [(dp, sub), (dp, 1 - sub)]
    for out, (half, which) in zip(outs, wanted):
        columns = pl.ds(pl.multiple_of((half * 2 + which) * quarter, LANES), quarter)
        for source, at in ((tokens, 0), (cotangent, quarter)):
            target = out.at[0:rows, at : at + quarter]
            copies.append(
                pltpu.make_async_copy(source.at[:, columns], target, sems.at[len(copies)])
            )
    for copy in copies:
        copy.start()
    parts, rest = [routes[:chosen]], routes[chosen:]
    for _ in range(3):
        part = rest.astype(BF).astype(F32)
        parts.append(part)
        rest = rest - part
    table = jnp.concatenate(parts, axis=0)
    per_row = 2 * quarter // rows
    lines = [
        jnp.concatenate([table[i : i + 1] for i in range(start, start + per_row)], axis=1)
        for start in range(0, 4 * chosen, per_row)
    ]
    lines.append(jnp.zeros((ROUTE_ROWS - len(lines), 2 * quarter), F32))
    lines = jnp.concatenate(lines, axis=0).astype(BF)
    for out in outs:
        out[rows:, :] = lines
    for copy in copies:
        copy.wait()


def pack(place, tokens, cotangent, route_ids, route_weights, wide, quarter):
    rows = route_ids.shape[0]
    shape = (rows + ROUTE_ROWS, 2 * quarter)
    routes = jnp.concatenate([route_ids.T.astype(F32), route_weights.T], axis=0)
    return pl.pallas_call(
        pack_kernel,
        in_specs=[SMEM] + [pl.BlockSpec(memory_space=pltpu.HBM)] * 2 + [WHOLE],
        out_specs=[WHOLE] * (wide + 1),
        out_shape=[jax.ShapeDtypeStruct(shape, BF)] * (wide + 1),
        scratch_shapes=[pltpu.SemaphoreType.DMA((2 * wide + 2,))],
        compiler_params=pltpu.CompilerParams(vmem_limit_bytes=LIMIT),
        cost_estimate=PACK_COST,
    )(place, tokens, cotangent, routes)


def route_tables(payloads, token_rows, chosen, first_expert, dp, local_experts, tables):
    shards = len(payloads)
    per_row = payloads[0].shape[1] // token_rows
    lines = [payload[token_rows:, :].astype(F32) for payload in payloads]

    def entry(index):
        row, column = divmod(index, per_row)
        at = slice(column * token_rows, (column + 1) * token_rows)
        return jnp.concatenate([line[row : row + 1, at] for line in lines], axis=1)

    ids = [entry(k) for k in range(chosen)]
    weights = [
        entry(chosen + k) + entry(2 * chosen + k) + entry(3 * chosen + k) for k in range(chosen)
    ]
    total = shards * token_rows
    masks, scales = [], []
    for local in range(local_experts):
        wanted = (first_expert + local).astype(F32)
        hits = [(one == wanted).astype(F32) for one in ids]
        masks.append(sum(hits))
        scales.append(sum(hit * weight for hit, weight in zip(hits, weights)))
    pad = [jnp.zeros((8 - local_experts, total), F32)] if local_experts < 8 else []
    mask = jnp.concatenate(masks + pad, axis=0)

    def number(axis):
        index = lax.broadcasted_iota(jnp.int32, (total, total), axis)
        part = sum((index >= i * token_rows).astype(jnp.int32) for i in range(1, shards + 1))
        shard = dp - part
        return index + (jnp.where(shard < 0, shard + shards, shard) - part) * token_rows

    rank = dot(mask.astype(BF), (number(0) < number(1)).astype(F32).astype(BF))
    tables[0:8, :] = jnp.where(mask > 0.5, rank, -1.0)
    tables[8:16, :] = jnp.concatenate(scales + pad, axis=0)


def one_hot(tables, local, slots):
    rank = tables[pl.ds(local, 1), :].astype(jnp.int32)
    total = rank.shape[1]
    return lax.broadcasted_iota(jnp.int32, (slots, total), 0) == rank


def forward_kernel(shards, token_rows, chosen, capacity, streamed, place, *refs):
    mine, other, refs = refs[:shards], refs[shards : 2 * shards], refs[2 * shards :]
    gate, up, down, _, sums, cot_rows, tables, token_scratch, sum_scratch = refs
    quarter = mine[0].shape[1] // 2
    experts = sums.shape[1] // capacity
    slots = cot_rows.shape[1]

    def routing():
        route_tables(mine, token_rows, chosen, place[1], place[2], experts, tables)

    def finish():
        sums[...] = sum_scratch[...].astype(BF)

    def one_expert(local, at):
        hot = one_hot(tables, local, slots).astype(F32).astype(BF)
        for source, which in ((mine, place[0]), (other, 1 - place[0])):
            rows = jnp.concatenate([one[0:token_rows, :] for one in source], axis=0)
            columns = pl.ds(pl.multiple_of(which * quarter, LANES), quarter)
            picked = dot(hot, rows).astype(BF)
            token_scratch[:, columns] = picked[:, :quarter]
            cot_rows[at, :, columns] = picked[:, quarter:]
        start = pl.multiple_of(local * capacity, 8) if streamed else local * capacity
        here = pl.ds(start, capacity)
        sum_scratch[0, here, :] = dot(token_scratch[...], gate[at])[:capacity]
        sum_scratch[1, here, :] = dot(token_scratch[...], up[at])[:capacity]
        sum_scratch[2, here, :] = dot(cot_rows[at], down[at], ((1,), (1,)))[:capacity]

    if streamed:
        local = pl.program_id(0)
        pl.when(local == 0)(routing)
        one_expert(local, 0)
        pl.when(local == experts - 1)(finish)
    else:
        routing()
        for local in range(experts):
            one_expert(local, local)
        finish()


def backward_kernel(capacity, parts, wide, place, *refs):
    tables, refs = refs[:parts], refs[parts:]
    sums, refs = refs[: parts * wide], refs[parts * wide :]
    gate, up, _, hidden, keep, send, full, total = refs
    rows = sums[0].shape[1]
    experts = hidden.shape[0]
    slots = hidden.shape[1] // parts
    quarter = keep.shape[1]
    for part in range(parts):
        here = sums[part * wide : (part + 1) * wide]
        full[part, :, 0:rows, :] = sum(one[...].astype(F32) for one in here)
        full[part, :, rows:, :] = jnp.zeros((3, full.shape[2] - rows, full.shape[3]), F32)
    for local in range(experts):
        gate_tokens, up_tokens = [], []
        for part in range(parts):
            hot = one_hot(tables[part], local, slots).astype(F32)
            scale = jnp.sum(hot * tables[part][8 + local : 9 + local, :], axis=1, keepdims=True)
            here = slice(local * capacity, local * capacity + slots)
            pre_gate, pre_up, tangent = (full[part, i, here, :] for i in range(3))
            sigmoid_gate = jax.nn.sigmoid(pre_gate)
            act = pre_gate * sigmoid_gate
            slope = sigmoid_gate * (1.0 + pre_gate * (1.0 - sigmoid_gate))
            hidden[local, part * slots : (part + 1) * slots, :] = (scale * act * pre_up).astype(BF)
            scaled = scale * tangent
            gate_adjoint = (scaled * pre_up * slope).astype(BF)
            up_adjoint = (scaled * act).astype(BF)
            hot = hot.astype(BF)
            gate_tokens.append(dot(hot, gate_adjoint, ((0,), (0,))).astype(BF))
            up_tokens.append(dot(hot, up_adjoint, ((0,), (0,))).astype(BF))
        gate_tokens = jnp.concatenate(gate_tokens, axis=0)
        up_tokens = jnp.concatenate(up_tokens, axis=0)
        term = dot(gate_tokens, gate[local], ((1,), (1,)))
        term = term + dot(up_tokens, up[local], ((1,), (1,)))
        total[...] = term if local == 0 else total[...] + term
    for out, which in ((keep, place[0]), (send, 1 - place[0])):
        out[...] = total[:, pl.ds(pl.multiple_of(which * quarter, LANES), quarter)].astype(BF)


def grad_kernel(half, *refs):
    *inputs, out, done = refs
    done[...] = jnp.zeros_like(done)
    local = pl.program_id(0)
    hidden = jnp.concatenate([one[local] for one in inputs[:half]], axis=0)
    cot_rows = jnp.concatenate([one[local] for one in inputs[half:]], axis=0)
    out[0] = dot(hidden, cot_rows, ((0,), (0,))).astype(BF)


SMEM = pl.BlockSpec(memory_space=pltpu.SMEM)
ANY = pl.BlockSpec(memory_space=pl.ANY)
WHOLE = pl.BlockSpec(memory_space=pltpu.VMEM)
LIMIT = 12 * 1024 * 1024
STREAM_LIMIT = 60 * 1024 * 1024
ROUTE_ROWS = 16
PACK_COST = pl.CostEstimate(flops=1, bytes_accessed=32 * 1024 * 1024, transcendentals=0)
NO_COST = pl.CostEstimate(flops=1, bytes_accessed=1, transcendentals=0)


def forward(
    place, mine, other, gate, up, down, token_rows, chosen, most, previous, streamed=False
):
    local_experts, depth, hidden = gate.shape
    shards = len(mine)
    capacity = up_to(shards * most, 8)
    slots = up_to(capacity, 16)
    rows = local_experts * capacity
    tokens = shards * token_rows
    weights = [WHOLE] * 3
    if streamed:
        weights = [expert_spec((depth, hidden))] * 2 + [expert_spec((hidden, depth))]
    return pl.pallas_call(
        functools.partial(forward_kernel, shards, token_rows, chosen, capacity, streamed),
        grid=(local_experts,) if streamed else (),
        in_specs=[SMEM] + [WHOLE] * (2 * shards) + weights + [ANY],
        out_specs=[WHOLE, expert_spec((slots, depth)) if streamed else WHOLE, WHOLE],
        out_shape=[
            jax.ShapeDtypeStruct((3, rows, hidden), BF),
            jax.ShapeDtypeStruct((local_experts, slots, depth), BF),
            jax.ShapeDtypeStruct((16, tokens), F32),
        ],
        scratch_shapes=[pltpu.VMEM((slots, depth), BF), pltpu.VMEM((3, rows, hidden), F32)],
        compiler_params=pltpu.CompilerParams(vmem_limit_bytes=STREAM_LIMIT if streamed else LIMIT),
        cost_estimate=NO_COST,
    )(place, *mine, *other, gate, up, down, previous)


def backward(place, tables, sums, gate, up, previous):
    local_experts, depth, hidden = gate.shape
    parts, wide = len(tables), len(sums[0])
    rows = sums[0][0].shape[1]
    capacity = rows // local_experts
    slots = up_to(capacity, 16)
    tokens = parts * tables[0].shape[1]
    flat = [one for part in sums for one in part]
    return pl.pallas_call(
        functools.partial(backward_kernel, capacity, parts, wide),
        in_specs=[SMEM] + [WHOLE] * (parts + len(flat) + 2) + [ANY],
        out_specs=[WHOLE] * 3,
        out_shape=[
            jax.ShapeDtypeStruct((local_experts, parts * slots, hidden), BF),
            jax.ShapeDtypeStruct((tokens, depth // 2), BF),
            jax.ShapeDtypeStruct((tokens, depth // 2), BF),
        ],
        scratch_shapes=[
            pltpu.VMEM((parts, 3, rows + slots - capacity + 8, hidden), F32),
            pltpu.VMEM((tokens, depth), F32),
        ],
        compiler_params=pltpu.CompilerParams(vmem_limit_bytes=LIMIT),
        cost_estimate=NO_COST,
    )(place, *tables, *flat, gate, up, previous)


def grads(hiddens, cots):
    local_experts, _, hidden = hiddens[0].shape
    depth = cots[0].shape[2]
    slots = sum(one.shape[1] for one in cots)
    return pl.pallas_call(
        functools.partial(grad_kernel, len(hiddens)),
        grid=(local_experts,),
        in_specs=[WHOLE] * (len(hiddens) + len(cots)),
        out_specs=[expert_spec((hidden, depth)), vmem_spec((8, LANES))],
        out_shape=[
            jax.ShapeDtypeStruct((local_experts, hidden, depth), BF),
            jax.ShapeDtypeStruct((8, LANES), F32),
        ],
        compiler_params=pltpu.CompilerParams(vmem_limit_bytes=LIMIT),
        cost_estimate=NO_COST,
    )(*hiddens, *cots)


def small(kernel, shapes, *arrays):
    return pl.pallas_call(
        kernel,
        in_specs=[SMEM] + [WHOLE] * (len(arrays) - 1),
        out_specs=[WHOLE] * len(shapes),
        out_shape=[jax.ShapeDtypeStruct(shape, BF) for shape in shapes],
        compiler_params=pltpu.CompilerParams(vmem_limit_bytes=LIMIT),
        cost_estimate=NO_COST,
    )(*arrays)


def sum_kernel(inputs, place, *refs):
    total = sum(one[...].astype(F32) for one in refs[:inputs]).astype(BF)
    rows = refs[inputs].shape[0]
    for index, out in enumerate(refs[inputs:]):
        out[...] = total[index * rows : (index + 1) * rows]


def turned_kernel(inputs, place, *refs):
    total = sum(one[...].astype(F32) for one in refs[:inputs]).astype(BF)
    first, second = refs[inputs:]
    rows = first.shape[0]
    straight = place[2] == place[0]

    @pl.when(straight)
    def _():
        first[...] = total[:rows]
        second[...] = total[rows:]

    @pl.when(jnp.logical_not(straight))
    def _():
        first[...] = total[rows:]
        second[...] = total[:rows]


def choose_kernel(place, one, two, stay, send):
    straight = place[2] == place[0]

    @pl.when(straight)
    def _():
        stay[...] = one[...]
        send[...] = two[...]

    @pl.when(jnp.logical_not(straight))
    def _():
        stay[...] = two[...]
        send[...] = one[...]


def final_kernel(place, stay, come, *refs):
    *far, out = refs
    quarter = stay.shape[1]

    def far_sum(flip):
        return [
            sum(far[start + (q + flip) % 2][...].astype(F32) for start in range(0, len(far), 2))
            for q in range(2)
        ]

    for sub in range(2):
        for dp in range(2):

            @pl.when((place[0] == sub) & (place[2] == dp))
            def _():
                own = [stay[...], come[...]] if sub == 0 else [come[...], stay[...]]
                for q, extra in enumerate(far_sum(dp)):
                    out[:, q * quarter : (q + 1) * quarter] = (own[q].astype(F32) + extra).astype(BF)


def shift(array, axis, by):
    size = lax.axis_size(axis)
    return lax.ppermute(array, axis, [(i, (i + by) % size) for i in range(size)])


def after(array, *done):
    return lax.optimization_barrier((array,) + done)[0]


def per_device(tokens, cotangent, route_ids, route_weights, w_gate, w_up, v_down):
    owners, wide, cores = (lax.axis_size(a) for a in ("expert", "dp", "sub"))
    owner, dp, sub = (lax.axis_index(a) for a in ("expert", "dp", "sub"))
    token_rows, chosen = route_ids.shape
    local_experts = w_gate.shape[0]
    expert_count = owners * local_experts
    most = max(2, 9 * token_rows * chosen // (8 * expert_count))
    quarter = tokens.shape[1] // (wide * cores)
    place = jnp.stack([sub, owner * local_experts, dp]).astype(jnp.int32)

    *sends, own, own_other = pack(
        place, tokens, cotangent, route_ids, route_weights, wide, quarter
    )

    def ahead(mine, other, previous, streamed=False):
        return forward(
            place, mine, other, w_gate, w_up, v_down, token_rows, chosen, most, previous, streamed
        )

    received = [shift(one, "dp", by) for by, one in enumerate(sends, 1)]
    parts = [ahead([own], [own_other], place)]
    blocks, swapped = [[own] + received], [[]]
    for by in range(1, owners):
        blocks.append([])
        for one in blocks[-2]:
            one = after(one, *blocks[-1]) if by == 2 else one
            blocks[-1].append(shift(one, "expert", 1))
    blocks.append([])
    swapped.append([shift(blocks[1][0], "sub", 1)])
    for one in received:
        other = shift(after(one, parts[0][2]), "sub", 1)
        previous = after(parts[-1][2], swapped[1][0])
        parts.append(ahead([one], [other], previous))
    home_sums = [[part[0]] for part in parts]
    arrived = []
    for index in range(wide):
        for step in range(1, wide):
            got = shift(parts[index][0], "dp", -step)
            home_sums[(index - step) % wide].append(got)
            arrived.append(got)
    hiddens, cots = [], [part[1] for part in parts]
    waiting = ([part[2] for part in parts], home_sums)
    last = parts[-1][2]
    swapped[1] += [
        shift(after(one, last, *arrived[: wide - 1]), "sub", 1) for one in blocks[1][1:]
    ]
    gate_for_sums = arrived[wide - 1 :]

    def behind(waiting, previous, crossing_after=()):
        hidden, keep, send = backward(place, *waiting, w_gate, w_up, previous)
        hiddens.append(hidden)
        send = after(send, *crossing_after)
        return hidden, (keep, shift(send, "sub", 1))

    direct = wide == cores
    near, far = [], []

    def sent_back(halves, by):
        if by < 2 or not direct:
            (rows,) = small(
                functools.partial(sum_kernel, 2), [halves[0].shape], place, *halves
            )
            near.append(shift(rows, "expert", -by) if by else rows)
            return [rows]
        pieces = small(
            functools.partial(turned_kernel, 2), [(token_rows, quarter)] * 2, place, *halves
        )
        return pieces

    def sent_straight(pieces, by):
        for way, piece in enumerate(pieces):
            pairs = []
            for index in range(owners * wide * cores):
                place_of, from_dp, from_sub = (
                    index // (wide * cores),
                    index // cores % wide,
                    index % cores,
                )
                to = (place_of - by) % owners * wide + (from_sub + way) % wide
                pairs.append((index, to * cores + from_dp))
            far.append(lax.ppermute(piece, ("expert", "dp", "sub"), pairs))

    def gathered(rows):
        pieces = jnp.zeros((wide, token_rows, quarter), BF)
        for by in range(wide):
            one = rows[by * token_rows : (by + 1) * token_rows].astype(BF)
            one = after(shift(one, "dp", -by), last) if by else one
            pieces = lax.dynamic_update_slice_in_dim(pieces, one[None], (dp + by) % wide, 0)
        span = wide // cores
        stay = lax.dynamic_slice_in_dim(pieces, sub * span, span, 0)
        come = shift(lax.dynamic_slice_in_dim(pieces, (1 - sub) * span, span, 0), "sub", 1)
        columns = []
        for index in range(span):
            columns.append(jnp.where(sub == 0, stay[index], come[index]))
            columns.append(jnp.where(sub == 0, come[index], stay[index]))
        return jnp.concatenate(columns, axis=1)

    for by in range(1, owners):
        sums, cot_rows, tables = ahead(blocks[by], swapped[by], last)
        cots.append(cot_rows)
        send = after(sums, *gate_for_sums)
        gate_for_sums = [shift(send, "dp", step) for step in range(1, wide)]
        last, halves = behind(waiting, tables)
        pieces = sent_back(halves, by - 1)
        if direct and by - 1 >= 2:
            sent_straight(pieces, by - 1)
        waiting = ([tables], [[sums] + gate_for_sums])
        swapped.append([])
        for one in blocks[by + 1]:
            one = after(one, last, *blocks[by + 1], *swapped[-1])
            swapped[-1].append(shift(one, "sub", 1))
    if not direct or owners < 3:
        last, halves = behind(waiting, after(last, *pieces))
        sent_back(halves, owners - 1)
        grad_down, _ = grads(hiddens, cots)
        return (grad_down, gathered(sum((one.astype(F32) for one in near[1:]), near[0])))
    last, halves = behind(waiting, after(last, *pieces), far)
    pieces = sent_back(halves, owners - 1)
    keep, send = small(
        functools.partial(sum_kernel, len(near)), [(token_rows, quarter)] * 2, place,
        *near[:-1], after(near[-1], last),
    )
    got = shift(send, "dp", -1)
    hiddens[-1], *pieces = lax.optimization_barrier((last, *pieces))
    sent_straight(pieces, owners - 1)
    grad_down, done = grads(hiddens, cots)
    stay, send = small(choose_kernel, [keep.shape] * 2, place, keep, got)
    come = shift(send, "sub", 1)
    far = [after(one, done) for one in far]
    (out,) = small(
        final_kernel, [(token_rows, cores * quarter)], place, stay, come, *far
    )
    return (grad_down, out)


def solution(mesh):
    placed = (
        P(("groups", "expert", "dp"), None),
        P(("groups", "expert", "dp"), None),
        P(("groups", "expert", "dp"), None),
        P(("groups", "expert", "dp"), None),
        P("expert", "dp", "sub"),
        P("expert", "dp", "sub"),
        P(("groups", "expert"), "sub", "dp"),
    )
    return jax.shard_map(
        per_device,
        mesh=mesh,
        in_specs=placed,
        out_specs=(P(("groups", "expert"), "sub", "dp"), P(("groups", "expert", "dp"), "sub")),
        check_vma=False,
    )
```
